32 devices in a mesh: ctx: 8 (over y, x, core), head: 4 (over z).
Axes of the slice: x: 2, y: 2, z: 4, core: 2. Of those that a mesh axis runs over, the one named last changes fastest.
Arguments:
- query_raw: bfloat16 [4096, 2048], P('ctx', 'head'), may hold values from -120 to 120
- key_raw: bfloat16 [4096, 2048], P('ctx', 'head'), may hold values from -120 to 120
- value_raw: bfloat16 [4096, 4096], P('ctx', 'head'), may hold values from -120 to 120
- conv_query: bfloat16 [4, 2048], P(None, 'head'), may hold values from -3 to 3
- conv_key: bfloat16 [4, 2048], P(None, 'head'), may hold values from -3 to 3
- conv_value: bfloat16 [4, 4096], P(None, 'head'), may hold values from -3 to 3
- decay_log: float32 [32, 4096], P('head', 'ctx'), may hold values from -0.6 to 0, as said below
- write_beta: float32 [32, 4096], P('head', 'ctx'), may hold values from 0 to 1
- gate_input: bfloat16 [4096, 4096], P('ctx', 'head'), may hold values from -6 to 6
- norm_gain: float32 [128], replicated, may hold values from 0.5 to 1.5
- out_weight: bfloat16 [4096, 2048], P('head'), may hold values from -0.125 to 0.125
Outputs:
- mixed: bfloat16 [4096, 2048], P('ctx', 'head')
The draws below stay inside these ranges and needn't reach their ends.
Inputs may be any that keep to these rules, and one draw needn't show every extreme that they name: `decay_log`: natural logarithm of a decay factor.
All inputs are finite; a program needn't handle non-finite values.
Results may differ from the reference program's by a relative error of at most 0.014.
Values may be sent and summed in bfloat16 or wider, within the bound.
A program may use at most 128 MiB of HBM per device.

```python
import math
import jax
import jax.numpy as jnp
from jax import lax

D_MODEL = 2048
HK = 16
VALUE_HEAD_COUNT = 32
DK = 128
DV = 128
CONV = 4
BLOCK = 64
TOK_DEV = 512
WINDOW_TOKENS = 4096
N_HEAD = 4


def gate_plan(key):
    parallel_lanes = jax.random.split(jax.random.fold_in(key, 31), 8)
    slow_share = 0.5
    gradual_heads = jax.random.uniform(parallel_lanes[0], (VALUE_HEAD_COUNT, 1)) < slow_share
    roughness = jax.random.uniform(parallel_lanes[1], (VALUE_HEAD_COUNT, WINDOW_TOKENS), minval=0.5, maxval=1.5)
    block_scale = jnp.exp(jax.random.uniform(parallel_lanes[2], (VALUE_HEAD_COUNT, WINDOW_TOKENS // TOK_DEV, 1), minval=math.log(0.5), maxval=math.log(2.0)))
    block_scale = jnp.broadcast_to(block_scale, (VALUE_HEAD_COUNT, WINDOW_TOKENS // TOK_DEV, TOK_DEV)).reshape(VALUE_HEAD_COUNT, WINDOW_TOKENS)
    fast_rate = jax.random.uniform(parallel_lanes[3], (VALUE_HEAD_COUNT, 1), minval=1.0 / 50.0, maxval=1.0 / 30.0)
    forget_speed = jnp.where(gradual_heads, 0.15 / WINDOW_TOKENS, fast_rate) * roughness * block_scale
    spike_positions = jax.random.randint(parallel_lanes[4], (3,), 0, WINDOW_TOKENS)
    spike_mask = jnp.any(jnp.arange(WINDOW_TOKENS)[None, :] == spike_positions[:, None], axis=0)[None, :] & gradual_heads
    spike_decrease = jnp.log(jax.random.uniform(parallel_lanes[5], (VALUE_HEAD_COUNT, WINDOW_TOKENS), minval=0.6, maxval=0.8))
    forget_factors = jnp.where(spike_mask, spike_decrease, -forget_speed)
    small_beta = 0.25 * DK / WINDOW_TOKENS * jax.random.uniform(parallel_lanes[6], (VALUE_HEAD_COUNT, WINDOW_TOKENS), minval=0.5, maxval=1.5)
    large_beta = jax.random.uniform(parallel_lanes[7], (VALUE_HEAD_COUNT, WINDOW_TOKENS), minval=0.3, maxval=0.9)
    beta_values = jnp.where(gradual_heads, jnp.minimum(small_beta, 0.5), large_beta)
    return (forget_factors, beta_values)


def draw_rows(key, width):
    parallel_lanes = jax.random.split(key, 3)
    row_scale = jnp.exp(jax.random.uniform(parallel_lanes[0], (WINDOW_TOKENS, 1), minval=0.0, maxval=math.log(10.0)))
    column_scale = jnp.exp(jax.random.uniform(parallel_lanes[1], (1, width), minval=math.log(0.5), maxval=math.log(2.0)))
    base_draw = jax.random.normal(parallel_lanes[2], (WINDOW_TOKENS, width))
    base_draw = jnp.clip(base_draw, -6.0, 6.0)
    return jnp.clip(base_draw * row_scale * column_scale, -120.0, 120.0)


def draw_query_raw(key, part):
    return draw_rows(jax.random.fold_in(key, 1), HK * DK).astype(jnp.bfloat16)


def draw_key_raw(key, part):
    return draw_rows(jax.random.fold_in(key, 2), HK * DK).astype(jnp.bfloat16)


def draw_value_raw(key, part):
    return draw_rows(jax.random.fold_in(key, 3), VALUE_HEAD_COUNT * DV).astype(jnp.bfloat16)


def draw_decay_log(key, part):
    return gate_plan(key)[0].astype(jnp.float32)


def draw_write_beta(key, part):
    return gate_plan(key)[1].astype(jnp.float32)


def spiked(values, own_key, source, target, shards_of, factor):
    owner, partner = [(jnp.arange(values.shape[position]) // (values.shape[position] // shards_of)).reshape([-1 if axis == position else 1 for axis in range(values.ndim)]) for position in (source, target)]
    chosen = jax.random.permutation(own_key, shards_of)[partner]
    strong = (owner == chosen) | (owner == (partner + shards_of // 2) % shards_of)
    return jnp.where(strong, factor * values, values)


def shard_levels(own_key, extent, cuts, smallest, top_value):
    def one(axis_at, parts):
        steps = jax.random.uniform(jax.random.fold_in(jax.random.fold_in(own_key, 6), axis_at), (parts,), jnp.float32, smallest / len(cuts), top_value / len(cuts))
        return jnp.repeat(jnp.exp(steps), extent[axis_at] // parts).reshape((-1,) + (1,) * (len(extent) - axis_at - 1))

    loudness = one(*cuts[0])
    for cut in cuts[1:]:
        loudness = loudness * one(*cut)
    return loudness


def centred(key, extent, deviation, reach, cuts=(), kind=jnp.bfloat16):
    values = deviation * jax.random.normal(key, extent, jnp.float32)
    if cuts:
        values = values * shard_levels(key, extent, cuts, -0.22, 0.18)
    return jnp.clip(values, -reach, reach).astype(kind)


def noise_with(rng, dims, scale, most, pieces, heavy, kind=jnp.bfloat16):
    values = scale * jax.random.normal(rng, dims, jnp.float32)
    if pieces:
        values = values * shard_levels(rng, dims, pieces, -0.22, 0.18)
    return jnp.clip(spiked(values, jax.random.fold_in(rng, 3), *heavy), -most, most).astype(kind)


def setup_inputs(seed: int = 0) -> dict:
    seeds = jax.random.split(jax.random.key(seed), 12)
    return {
        "query_raw": draw_query_raw(jax.random.fold_in(seeds[11], 71), 0),
        "key_raw": draw_key_raw(jax.random.fold_in(seeds[11], 71), 0),
        "value_raw": draw_value_raw(jax.random.fold_in(seeds[11], 71), 0),
        "conv_query": centred(seeds[3], (CONV, HK * DK), 0.5, 3.0, ((1, 4),)),
        "conv_key": centred(seeds[4], (CONV, HK * DK), 0.5, 3.0, ((1, 4),)),
        "conv_value": centred(seeds[5], (CONV, VALUE_HEAD_COUNT * DV), 0.5, 3.0, ((1, 4),)),
        "decay_log": draw_decay_log(jax.random.fold_in(seeds[11], 71), 0),
        "write_beta": draw_write_beta(jax.random.fold_in(seeds[11], 71), 0),
        "gate_input": centred(seeds[8], (WINDOW_TOKENS, VALUE_HEAD_COUNT * DV), 1.0, 6.0, ((0, 8), (1, 4))),
        "norm_gain": jnp.clip(jax.random.uniform(seeds[9], (DV,), jnp.float32, 0.5, 1.5), 0.5, 1.5),
        "out_weight": noise_with(seeds[10], (VALUE_HEAD_COUNT * DV, D_MODEL), (VALUE_HEAD_COUNT * DV) ** -0.5, 0.125, ((0, 4),), (0, 1, 4, 2.0)),
    }


highest = lax.Precision.HIGHEST

def conv_silu(raw_rows, conv_weight):
    widths = conv_weight.shape[0]
    length = raw_rows.shape[0]
    padded = jnp.concatenate([jnp.zeros((widths - 1, raw_rows.shape[1]), jnp.float32), raw_rows.astype(jnp.float32)], 0)
    weights = conv_weight.astype(jnp.float32)
    running = jnp.zeros((length, raw_rows.shape[1]), jnp.float32)
    for offset in range(widths):
        running = running + weights[offset] * padded[offset:offset + length]
    return jax.nn.silu(running)

def unit_rows(values):
    return values * lax.rsqrt(lax.optimization_barrier(jnp.sum(values * values, -1, keepdims=True)) + 1e-06)

def prepare(key_block, value_block, cumulative, beta_blocks):
    length = key_block.shape[-2]
    inner_keys = jnp.einsum('...id,...jd->...ij', key_block, key_block, precision=highest)
    positions = jnp.arange(length)
    strict_lower = positions[:, None] > positions[None, :]
    causal = positions[:, None] >= positions[None, :]
    spread = jnp.exp(jnp.where(causal, cumulative[..., :, None] - cumulative[..., None, :], 0.0))
    lower_part = jnp.where(strict_lower, beta_blocks[..., :, None] * inner_keys * spread, 0.0)
    system = jnp.eye(length, dtype=jnp.float32) + lower_part
    key_mix = jax.scipy.linalg.solve_triangular(system, (beta_blocks * jnp.exp(cumulative))[..., None] * key_block, lower=True)
    value_mix = jax.scipy.linalg.solve_triangular(system, beta_blocks[..., None] * value_block, lower=True)
    return (key_mix, value_mix, spread, causal)

def block_outputs(carry_state, query_block, key_block, key_mix, value_mix, cumulative, spread, causal):
    fresh_values = value_mix - jnp.einsum('hcd,hvd->hcv', key_mix, carry_state, precision=highest)
    scores = jnp.where(causal, jnp.einsum('hid,hjd->hij', query_block, key_block, precision=highest) * spread, 0.0)
    result = jnp.einsum('hcd,hvd->hcv', query_block * jnp.exp(cumulative)[..., None], carry_state, precision=highest)
    result = result + jnp.einsum('hij,hjv->hiv', scores, fresh_values, precision=highest)
    last_cum = cumulative[:, -1]
    carried = jnp.exp(last_cum[:, None] - cumulative)[..., None] * fresh_values
    carry_state = jnp.exp(last_cum)[:, None, None] * carry_state + jnp.einsum('hcv,hcd->hvd', carried, key_block, precision=highest)
    return (carry_state, result)

def reference(query_raw, key_raw, value_raw, conv_query, conv_key, conv_value, decay_log, write_beta, gate_input, norm_gain, out_weight):
    head_ratio = VALUE_HEAD_COUNT // HK
    block_count = WINDOW_TOKENS // BLOCK
    queries = unit_rows(conv_silu(query_raw, conv_query).reshape(WINDOW_TOKENS, HK, DK)) * DK ** (-0.5)
    key_unit = unit_rows(conv_silu(key_raw, conv_key).reshape(WINDOW_TOKENS, HK, DK))
    values = conv_silu(value_raw, conv_value).reshape(WINDOW_TOKENS, VALUE_HEAD_COUNT, DV)

    def blocks(array, heads, width):
        return array.reshape(block_count, BLOCK, heads, width).transpose(0, 2, 1, 3)
    cumulative = jnp.cumsum(decay_log.reshape(VALUE_HEAD_COUNT, block_count, BLOCK).transpose(1, 0, 2), axis=-1)
    beta_blocks = write_beta.reshape(VALUE_HEAD_COUNT, block_count, BLOCK).transpose(1, 0, 2)

    def advance(carry_state, inputs):
        query_block, key_block, value_block, cumul_block, beta_block = inputs
        query_block = jnp.repeat(query_block, head_ratio, axis=0)
        key_block = jnp.repeat(key_block, head_ratio, axis=0)
        key_mix, value_mix, spread, causal = prepare(key_block, value_block, cumul_block, beta_block)
        return block_outputs(carry_state, query_block, key_block, key_mix, value_mix, cumul_block, spread, causal)
    initial = jnp.zeros((VALUE_HEAD_COUNT, DV, DK), jnp.float32)
    unused, outputs = lax.scan(advance, initial, (blocks(queries, HK, DK), blocks(key_unit, HK, DK), blocks(values, VALUE_HEAD_COUNT, DV), cumulative, beta_blocks))
    heads_out = outputs.transpose(0, 2, 1, 3).reshape(WINDOW_TOKENS, VALUE_HEAD_COUNT, DV)
    normed = heads_out * lax.rsqrt(lax.optimization_barrier(jnp.mean(heads_out * heads_out, -1, keepdims=True)) + 1e-06)
    gated = normed * norm_gain * jax.nn.silu(gate_input.astype(jnp.float32).reshape(WINDOW_TOKENS, VALUE_HEAD_COUNT, DV))
    hidden = gated.astype(jnp.bfloat16).reshape(WINDOW_TOKENS, VALUE_HEAD_COUNT * DV)
    group_width = VALUE_HEAD_COUNT * DV // N_HEAD
    running = jnp.zeros((WINDOW_TOKENS, D_MODEL), jnp.float32)
    for member in range(N_HEAD):
        partial_sum = jnp.dot(hidden[:, member * group_width:(member + 1) * group_width].astype(jnp.float32), out_weight[member * group_width:(member + 1) * group_width].astype(jnp.float32), preferred_element_type=jnp.float32)
        rounded = lax.optimization_barrier(partial_sum.astype(jnp.bfloat16))
        running = running + rounded.astype(jnp.float32)
    return running.astype(jnp.bfloat16)
```

```python
import functools

import jax
import jax.numpy as jnp
from jax import lax
from jax.experimental import pallas as pl
from jax.experimental.pallas import tpu as pltpu
from jax.sharding import PartitionSpec as P

DK = 128
DV = 128
CONV = 4
BLOCK = 64
CHUNK = 2 * BLOCK
RIM = 16
F32 = jnp.float32
BF16 = jnp.bfloat16


def mm(a, b):
    return jnp.dot(a.astype(BF16), b.astype(BF16), preferred_element_type=F32)


def mm_nt(a, b):
    return lax.dot_general(
        a.astype(BF16), b.astype(BF16), (((1,), (1,)), ((), ())), preferred_element_type=F32
    )


def silu(x):
    return x / (1.0 + jnp.exp(-x))


def iota(shape, dim):
    return lax.broadcasted_iota(jnp.int32, shape, dim)


def conv_part(tail, rows, taps):
    whole = jnp.concatenate([tail, rows], 0)
    first = 8 - (CONV - 1)
    total = taps[0:1] * whole[first : first + CHUNK]
    for j in range(1, CONV):
        total = total + taps[j : j + 1] * whole[first + j : first + j + CHUNK]
    return silu(total)


def unit(x, scale):
    return x * (lax.rsqrt(jnp.sum(x * x, -1, keepdims=True) + 1e-06) * scale)


def local_kernel(
    q_ref, k_ref, v_ref, rim_ref, cq_ref, ck_ref, cv_ref, dec_ref, beta_ref,
    out_ref, qeff_ref, trans_ref,
    tail_ref, bd_ref, st_ref,
):
    tokens = q_ref.shape[0]
    key_heads = q_ref.shape[1] // DK
    heads = v_ref.shape[1] // DV
    ratio = heads // key_heads
    width = ratio * CHUNK
    qc, kc = q_ref.shape[1], k_ref.shape[1]

    tail_ref[...] = rim_ref[...].astype(F32)[RIM - 8 :]
    bd_ref[...] = (
        iota((width, width), 0) // BLOCK == iota((width, width), 1) // BLOCK
    ).astype(F32).astype(BF16)
    for h in range(heads):
        st_ref[h] = jnp.concatenate(
            [jnp.zeros((DK, DV), F32), (iota((DK, DK), 0) == iota((DK, DK), 1)).astype(F32)], 1
        )

    def diag(value):
        return jnp.concatenate([value] * (width // BLOCK), 0) * bd_ref[...]

    def step(c, unused):
        at = pl.ds(pl.multiple_of(c * CHUNK, CHUNK), CHUNK)
        row = iota((BLOCK, width), 0)
        lane = iota((BLOCK, width), 1)
        col = lane % BLOCK
        half = iota((BLOCK, CHUNK), 1) < BLOCK
        row1, col1 = iota((BLOCK, CHUNK), 0), iota((BLOCK, CHUNK), 1) % BLOCK
        eye = (row == col).astype(F32)

        dec = dec_ref[:, at]
        beta = beta_ref[:, at]
        tri = (
            (iota((CHUNK, CHUNK), 0) <= iota((CHUNK, CHUNK), 1))
            & (iota((CHUNK, CHUNK), 0) // BLOCK == iota((CHUNK, CHUNK), 1) // BLOCK)
        ).astype(F32)
        cum = jnp.dot(dec, tri, precision=lax.Precision.HIGHEST, preferred_element_type=F32)
        last = jnp.where(
            iota((heads, CHUNK), 1) < BLOCK, cum[:, BLOCK - 1 : BLOCK], cum[:, CHUNK - 1 : CHUNK]
        )
        grow = jnp.exp(cum)
        rows = jnp.concatenate(
            [cum, beta, beta * grow, grow, jnp.exp(last - cum)], 0
        )
        cols = jnp.transpose(
            jnp.concatenate([rows, jnp.zeros((CHUNK - rows.shape[0], CHUNK), F32)], 0)
        )

        def column(kind, h):
            return cols[:, kind * heads + h : kind * heads + h + 1]

        def compact(x):
            return jnp.where(half, x[:BLOCK], x[BLOCK:])

        def conv(ref, taps_ref, offset, part):
            s = pl.ds(part * DK, DK)
            t = pl.ds(offset + part * DK, DK)
            new = ref[at, s].astype(F32)
            result = conv_part(tail_ref[:, t], new, taps_ref[:, s].astype(F32))
            tail_ref[:, t] = new[CHUNK - 8 :]
            return result

        queries, keys, lowers, scores, values = [], [], [], [], []
        for kh in range(key_heads):
            q = unit(conv(q_ref, cq_ref, 0, kh), DK ** (-0.5))
            k = unit(conv(k_ref, ck_ref, qc, kh), 1.0)
            kk = compact(mm_nt(k, k))
            qk = compact(mm_nt(q, k))
            low = []
            for g in range(ratio):
                h = kh * ratio + g
                values.append(conv(v_ref, cv_ref, qc + kc, h))
                cc = compact(jnp.broadcast_to(column(0, h), (CHUNK, CHUNK)))
                bc = compact(jnp.broadcast_to(column(1, h), (CHUNK, CHUNK)))
                spread = jnp.exp(jnp.where(row1 >= col1, cc - cum[h : h + 1], 0.0))
                low.append(jnp.where(row1 > col1, bc * kk * spread, 0.0))
                scores.append(jnp.where(row1 >= col1, qk * spread, 0.0).astype(BF16))
            lowers.append(jnp.concatenate(low, 1))
            queries.append(q)
            keys.append(k)

        inverse = [eye - jnp.where(row // 2 == col // 2, low, 0.0) for low in lowers]
        size = 2
        while size < BLOCK:
            off = (row // (2 * size) == col // (2 * size)) & (row // size > col // size)
            left = [
                mm(x, diag(jnp.where(off, low, 0.0).astype(BF16)))
                for x, low in zip(inverse, lowers)
            ]
            inverse = [x - mm(p, diag(x.astype(BF16))) for x, p in zip(inverse, left)]
            size *= 2

        mixes = []
        for kh in range(key_heads):
            rhs = []
            for g in range(ratio):
                h = kh * ratio + g
                rhs.append(
                    jnp.concatenate([column(2, h) * keys[kh], column(1, h) * values[h]], 1)
                )
            mixes.append(mm(diag(inverse[kh].astype(BF16)), jnp.concatenate(rhs, 0)))

        firsts, seconds = [], []
        for h in range(heads):
            kh, g = h // ratio, h % ratio
            firsts.append((column(3, h) * queries[kh]).astype(BF16))
            turned = jnp.transpose(column(4, h) * keys[kh]).astype(BF16)
            seconds.append(jnp.concatenate([scores[h], turned], 0))

        for s in range(CHUNK // BLOCK):
            one = []
            for h in range(heads):
                kh, g = h // ratio, h % ratio
                mix = mixes[kh][g * CHUNK + s * BLOCK : g * CHUNK + (s + 1) * BLOCK]
                lhs = jnp.concatenate(
                    [mix[:, :DK].astype(BF16), firsts[h][s * BLOCK : (s + 1) * BLOCK]], 0
                )
                one.append((mm(lhs, st_ref[h]), mix[:, DK:]))
            for h in range(heads):
                r1, u = one[h]
                fresh = jnp.concatenate([u - r1[:BLOCK, :DV], -r1[:BLOCK, DV:]], 1).astype(BF16)
                zero = jnp.zeros_like(fresh)
                r2 = mm(seconds[h], jnp.concatenate([fresh, zero] if s == 0 else [zero, fresh], 0))
                result = r1[BLOCK:] + r2[:BLOCK]
                where = pl.ds(pl.multiple_of(c * CHUNK + s * BLOCK, BLOCK), BLOCK)
                out_ref[where, h * DV : (h + 1) * DV] = result[:, :DV]
                qeff_ref[where, h * DK : (h + 1) * DK] = result[:, DV:].astype(BF16)
                decay = jnp.exp(cum[h : h + 1, (s + 1) * BLOCK - 1 : (s + 1) * BLOCK])
                st_ref[h] = decay * st_ref[h] + r2[BLOCK:]
        return unused

    lax.fori_loop(0, tokens // CHUNK, step, 0)
    trans_ref[...] = st_ref[...].astype(BF16)


def finish_kernel(
    out_ref, qeff_ref, every_ref, gate_ref, gain_ref, weight_ref, part_ref, start_ref, hid_ref
):
    heads = every_ref.shape[1]
    tokens = out_ref.shape[0]
    place = lax.axis_index("ctx")
    start_ref[...] = jnp.zeros_like(start_ref)

    def lap(i, unused):
        for h in range(heads):
            state = start_ref[h]
            high = state.astype(BF16)
            low = (state - high.astype(F32)).astype(BF16)
            moved = mm(every_ref[i, h, :, DV:], jnp.concatenate([high, low], 1))
            start_ref[h] = moved[:, :DV] + moved[:, DV:] + every_ref[i, h, :, :DV].astype(F32)
        return unused

    lax.fori_loop(0, place, lap, 0)
    gain = gain_ref[...]
    rows = 128

    def chunk(c, unused):
        at = pl.ds(pl.multiple_of(c * rows, rows), rows)
        for h in range(heads):
            cs = slice(h * DV, (h + 1) * DV)
            o = out_ref[at, cs] + mm(qeff_ref[at, cs], start_ref[h])
            n = o * lax.rsqrt(jnp.mean(o * o, -1, keepdims=True) + 1e-06)
            hid_ref[at, cs] = (n * gain * silu(gate_ref[at, cs].astype(F32))).astype(BF16)
        hidden = hid_ref[at, :]
        width = part_ref.shape[2]
        for d in range(part_ref.shape[0]):
            part_ref[d, at, :] = mm(hidden, weight_ref[:, d * width : (d + 1) * width]).astype(BF16)
        return unused

    lax.fori_loop(0, tokens // rows, chunk, 0)


def body(
    query_raw, key_raw, value_raw, conv_query, conv_key, conv_value,
    decay_log, write_beta, gate_input, norm_gain, out_weight,
):
    tokens = query_raw.shape[0]
    heads = value_raw.shape[1] // DV
    ratio = value_raw.shape[1] // key_raw.shape[1]
    channels = query_raw.shape[1] + key_raw.shape[1] + value_raw.shape[1]
    n_ctx, n_head = lax.axis_size("ctx"), lax.axis_size("head")
    rim = lax.ppermute(
        jnp.concatenate([x[tokens - RIM :] for x in (query_raw, key_raw, value_raw)], 1),
        "ctx",
        [(i, i + 1) for i in range(n_ctx - 1)],
    )
    vmem = pl.BlockSpec(memory_space=pltpu.VMEM)
    out, qeff, trans = pl.pallas_call(
        local_kernel,
        out_shape=(
            jax.ShapeDtypeStruct((tokens, heads * DV), F32),
            jax.ShapeDtypeStruct((tokens, heads * DK), BF16),
            jax.ShapeDtypeStruct((heads, DK, DV + DK), BF16),
        ),
        in_specs=[vmem] * 9,
        out_specs=[vmem] * 3,
        scratch_shapes=[
            pltpu.VMEM((8, channels), F32),
            pltpu.VMEM((ratio * CHUNK, ratio * CHUNK), BF16),
            pltpu.VMEM((heads, DK, DV + DK), F32),
        ],
        compiler_params=pltpu.CompilerParams(vmem_limit_bytes=48 * 2**20),
        name="local",
    )(
        query_raw, key_raw, value_raw, rim, conv_query, conv_key, conv_value,
        decay_log, write_beta,
    )
    every = lax.all_gather(trans, "ctx")
    part = pl.pallas_call(
        finish_kernel,
        out_shape=jax.ShapeDtypeStruct((n_head, tokens, out_weight.shape[1] // n_head), BF16),
        in_specs=[vmem] * 6,
        out_specs=vmem,
        scratch_shapes=[
            pltpu.VMEM((heads, DK, DV), F32),
            pltpu.VMEM((tokens, heads * DV), BF16),
        ],
        compiler_params=pltpu.CompilerParams(vmem_limit_bytes=48 * 2**20),
        name="finish",
    )(out, qeff, every, gate_input, norm_gain.reshape(1, DV), out_weight)
    return lax.psum_scatter(part, "head", scatter_dimension=0)


def solution(mesh):
    return jax.shard_map(
        body,
        mesh=mesh,
        in_specs=(
            P("ctx", "head"), P("ctx", "head"), P("ctx", "head"),
            P(None, "head"), P(None, "head"), P(None, "head"),
            P("head", "ctx"), P("head", "ctx"), P("ctx", "head"),
            P(), P("head", None),
        ),
        out_specs=P("ctx", "head"),
        check_vma=False,
    )
```

```python
import functools

import jax
import jax.numpy as jnp
from jax import lax
from jax.experimental import pallas as pl
from jax.experimental.pallas import tpu as pltpu
from jax.sharding import PartitionSpec as P

DK = 128
DV = 128
CONV = 4
BLOCK = 64
CHUNK = 2 * BLOCK
RIM = 16
F32 = jnp.float32
BF16 = jnp.bfloat16


def mm(a, b):
    return jnp.dot(a.astype(BF16), b.astype(BF16), preferred_element_type=F32)


def mm_nt(a, b):
    return lax.dot_general(
        a.astype(BF16), b.astype(BF16), (((1,), (1,)), ((), ())), preferred_element_type=F32
    )


def silu(x):
    return x / (1.0 + jnp.exp(-x))


def iota(shape, dim):
    return lax.broadcasted_iota(jnp.int32, shape, dim)


def conv_part(tail, rows, taps):
    whole = jnp.concatenate([tail, rows], 0)
    first = 8 - (CONV - 1)
    total = taps[0:1] * whole[first : first + CHUNK]
    for j in range(1, CONV):
        total = total + taps[j : j + 1] * whole[first + j : first + j + CHUNK]
    return silu(total)


def unit(x, scale):
    return x * (lax.rsqrt(jnp.sum(x * x, -1, keepdims=True) + 1e-06) * scale)


def local_kernel(
    q_ref, k_ref, v_ref, rim_ref, cq_ref, ck_ref, cv_ref, dec_ref, beta_ref,
    out_ref, qeff_ref, trans_ref,
    tail_ref, bd_ref, st_ref,
):
    tokens = q_ref.shape[0]
    key_heads = q_ref.shape[1] // DK
    heads = v_ref.shape[1] // DV
    ratio = heads // key_heads
    width = ratio * CHUNK
    qc, kc = q_ref.shape[1], k_ref.shape[1]

    tail_ref[...] = rim_ref[...].astype(F32)[RIM - 8 :]
    bd_ref[...] = (
        iota((width, width), 0) // BLOCK == iota((width, width), 1) // BLOCK
    ).astype(F32).astype(BF16)
    for h in range(heads):
        st_ref[h] = jnp.concatenate(
            [jnp.zeros((DK, DV), F32), (iota((DK, DK), 0) == iota((DK, DK), 1)).astype(F32)], 1
        )

    def diag(value):
        return jnp.concatenate([value] * (width // BLOCK), 0) * bd_ref[...]

    def step(c, unused):
        at = pl.ds(pl.multiple_of(c * CHUNK, CHUNK), CHUNK)
        row = iota((BLOCK, width), 0)
        lane = iota((BLOCK, width), 1)
        col = lane % BLOCK
        half = iota((BLOCK, CHUNK), 1) < BLOCK
        row1, col1 = iota((BLOCK, CHUNK), 0), iota((BLOCK, CHUNK), 1) % BLOCK
        eye = (row == col).astype(F32)

        dec = dec_ref[:, at]
        beta = beta_ref[:, at]
        tri = (
            (iota((CHUNK, CHUNK), 0) <= iota((CHUNK, CHUNK), 1))
            & (iota((CHUNK, CHUNK), 0) // BLOCK == iota((CHUNK, CHUNK), 1) // BLOCK)
        ).astype(F32)
        cum = jnp.dot(dec, tri, precision=lax.Precision.HIGHEST, preferred_element_type=F32)
        last = jnp.where(
            iota((heads, CHUNK), 1) < BLOCK, cum[:, BLOCK - 1 : BLOCK], cum[:, CHUNK - 1 : CHUNK]
        )
        grow = jnp.exp(cum)
        rows = jnp.concatenate(
            [cum, beta, beta * grow, grow, jnp.exp(last - cum)], 0
        )
        cols = jnp.transpose(
            jnp.concatenate([rows, jnp.zeros((CHUNK - rows.shape[0], CHUNK), F32)], 0)
        )

        def column(kind, h):
            return cols[:, kind * heads + h : kind * heads + h + 1]

        def compact(x):
            return jnp.where(half, x[:BLOCK], x[BLOCK:])

        def conv(ref, taps_ref, offset, part):
            s = pl.ds(part * DK, DK)
            t = pl.ds(offset + part * DK, DK)
            new = ref[at, s].astype(F32)
            result = conv_part(tail_ref[:, t], new, taps_ref[:, s].astype(F32))
            tail_ref[:, t] = new[CHUNK - 8 :]
            return result

        queries, keys, lowers, scores, values = [], [], [], [], []
        for kh in range(key_heads):
            q = unit(conv(q_ref, cq_ref, 0, kh), DK ** (-0.5))
            k = unit(conv(k_ref, ck_ref, qc, kh), 1.0)
            kk = compact(mm_nt(k, k))
            qk = compact(mm_nt(q, k))
            low = []
            for g in range(ratio):
                h = kh * ratio + g
                values.append(conv(v_ref, cv_ref, qc + kc, h))
                cc = compact(jnp.broadcast_to(column(0, h), (CHUNK, CHUNK)))
                bc = compact(jnp.broadcast_to(column(1, h), (CHUNK, CHUNK)))
                spread = jnp.exp(jnp.where(row1 >= col1, cc - cum[h : h + 1], 0.0))
                low.append(jnp.where(row1 > col1, bc * kk * spread, 0.0))
                scores.append(jnp.where(row1 >= col1, qk * spread, 0.0).astype(BF16))
            lowers.append(jnp.concatenate(low, 1))
            queries.append(q)
            keys.append(k)

        inverse = [eye - jnp.where(row // 2 == col // 2, low, 0.0) for low in lowers]
        size = 2
        while size < BLOCK:
            off = (row // (2 * size) == col // (2 * size)) & (row // size > col // size)
            left = [
                mm(x, diag(jnp.where(off, low, 0.0).astype(BF16)))
                for x, low in zip(inverse, lowers)
            ]
            inverse = [x - mm(p, diag(x.astype(BF16))) for x, p in zip(inverse, left)]
            size *= 2

        mixes = []
        for kh in range(key_heads):
            rhs = []
            for g in range(ratio):
                h = kh * ratio + g
                rhs.append(
                    jnp.concatenate([column(2, h) * keys[kh], column(1, h) * values[h]], 1)
                )
            mixes.append(mm(diag(inverse[kh].astype(BF16)), jnp.concatenate(rhs, 0)))

        firsts, seconds = [], []
        for h in range(heads):
            kh, g = h // ratio, h % ratio
            firsts.append((column(3, h) * queries[kh]).astype(BF16))
            turned = jnp.transpose(column(4, h) * keys[kh]).astype(BF16)
            seconds.append(jnp.concatenate([scores[h], turned], 0))

        for s in range(CHUNK // BLOCK):
            one = []
            for h in range(heads):
                kh, g = h // ratio, h % ratio
                mix = mixes[kh][g * CHUNK + s * BLOCK : g * CHUNK + (s + 1) * BLOCK]
                lhs = jnp.concatenate(
                    [mix[:, :DK].astype(BF16), firsts[h][s * BLOCK : (s + 1) * BLOCK]], 0
                )
                one.append((mm(lhs, st_ref[h]), mix[:, DK:]))
            for h in range(heads):
                r1, u = one[h]
                fresh = jnp.concatenate([u - r1[:BLOCK, :DV], -r1[:BLOCK, DV:]], 1).astype(BF16)
                zero = jnp.zeros_like(fresh)
                r2 = mm(seconds[h], jnp.concatenate([fresh, zero] if s == 0 else [zero, fresh], 0))
                result = r1[BLOCK:] + r2[:BLOCK]
                where = pl.ds(pl.multiple_of(c * CHUNK + s * BLOCK, BLOCK), BLOCK)
                out_ref[where, h * DV : (h + 1) * DV] = result[:, :DV]
                qeff_ref[where, h * DK : (h + 1) * DK] = result[:, DV:].astype(BF16)
                decay = jnp.exp(cum[h : h + 1, (s + 1) * BLOCK - 1 : (s + 1) * BLOCK])
                st_ref[h] = decay * st_ref[h] + r2[BLOCK:]
        return unused

    lax.fori_loop(0, tokens // CHUNK, step, 0)
    trans_ref[...] = st_ref[...].astype(BF16)


def compose(later, earlier):
    moved = mm(later[:, DV:], earlier)
    return jnp.concatenate([moved[:, :DV] + later[:, :DV], moved[:, DV:]], 1)


def finish_kernel(
    bits, n_head, steps,
    out_ref, qeff_ref, trans_ref, gate_ref, gain_ref, weight_ref, mixed_ref,
    start_ref, hid_ref, total_ref, prefix_ref, low_ref, give_ref, got_ref, give_b_ref, got_b_ref,
    give_s_ref, part_ref, up_ref, down_ref,
    state_send, state_recv, part_send, up_recv, down_recv,
):
    heads = trans_ref.shape[0]
    own = heads // 2
    tokens = out_ref.shape[0]
    rows = tokens // steps
    width = mixed_ref.shape[1]
    me, z = lax.axis_index("ctx"), lax.axis_index("head")
    core = me % 2
    first, other = core * own, (1 - core) * own

    def bit(b):
        return (me // 2**b) % 2

    def partner(b):
        return {"ctx": me + (1 - 2 * bit(b)) * 2**b}

    barrier = pltpu.get_barrier_semaphore()
    for b in range(bits):
        pl.semaphore_signal(
            barrier, inc=1, device_id=partner(b), device_id_type=pl.DeviceIdType.MESH
        )

    @pl.when(z > 0)
    def _():
        pl.semaphore_signal(
            barrier, inc=1, device_id={"head": z - 1}, device_id_type=pl.DeviceIdType.MESH
        )

    @pl.when(z < n_head - 1)
    def _():
        pl.semaphore_signal(
            barrier, inc=1, device_id={"head": z + 1}, device_id_type=pl.DeviceIdType.MESH
        )

    inner = (z > 0) & (z < n_head - 1)

    @pl.when(inner)
    def _():
        pl.semaphore_wait(barrier, bits + 2)

    @pl.when(jnp.logical_not(inner))
    def _():
        pl.semaphore_wait(barrier, bits + 1)

    def state_copy(b, i):
        if b == 0:
            src, dst = trans_ref.at[other + i], got_ref.at[0, i]
        elif b == bits:
            src, dst = give_s_ref.at[i], start_ref.at[first + i]
        elif b == bits - 1:
            src, dst = give_b_ref.at[i], got_b_ref.at[i]
        else:
            src, dst = give_ref.at[b, i], got_ref.at[b, i]
        return pltpu.make_async_remote_copy(
            src_ref=src, dst_ref=dst, send_sem=state_send.at[b, i], recv_sem=state_recv.at[b, i],
            device_id=partner(0 if b == bits else b), device_id_type=pl.DeviceIdType.MESH,
        )

    for i in range(own):
        state_copy(0, i).start()
    fresh = jnp.concatenate(
        [jnp.zeros((DK, DV), F32), (iota((DK, DK), 0) == iota((DK, DK), 1)).astype(F32)], 1
    )
    for i in range(own):
        state_copy(0, i).wait_recv()
        mine = trans_ref[first + i].astype(F32)
        got = got_ref[0, i].astype(F32)
        low = jnp.where(core == 0, mine, got)
        total = compose(jnp.where(core == 0, got, mine), low)
        low_ref[i] = low
        total_ref[i] = total
        prefix_ref[i] = fresh
        if bits - 1 == 1:
            give_b_ref[i] = total[:, :DV].astype(BF16)
        else:
            give_ref[1, i] = total.astype(BF16)
        state_copy(1, i).start()
    for b in range(1, bits - 1):
        for i in range(own):
            state_copy(b, i).wait_recv()
            got = got_ref[b, i].astype(F32)
            total = total_ref[i]

            @pl.when(bit(b) == 1)
            def _():
                prefix_ref[i] = compose(prefix_ref[i], got)

            total = compose(
                jnp.where(bit(b) == 1, total, got), jnp.where(bit(b) == 1, got, total)
            )
            total_ref[i] = total
            if b + 1 == bits - 1:
                give_b_ref[i] = total[:, :DV].astype(BF16)
            else:
                give_ref[b + 1, i] = total.astype(BF16)
            state_copy(b + 1, i).start()
    for i in range(own):
        state_copy(bits - 1, i).wait_recv()
        prefix = prefix_ref[i]
        moved = mm(prefix[:, DV:], got_b_ref[i]) + prefix[:, :DV]
        chip = jnp.where(bit(bits - 1) == 1, moved, prefix[:, :DV])
        low = low_ref[i]
        later = mm(low[:, DV:], chip) + low[:, :DV]
        start_ref[first + i] = jnp.where(core == 0, chip, later).astype(BF16)
        give_s_ref[i] = jnp.where(core == 0, later, chip).astype(BF16)
        state_copy(bits, i).start()
    for i in range(own):
        pltpu.make_async_remote_copy(
            src_ref=give_s_ref.at[i], dst_ref=start_ref.at[other + i],
            send_sem=state_send.at[bits, i], recv_sem=state_recv.at[bits, i],
            device_id=partner(0), device_id_type=pl.DeviceIdType.MESH,
        ).wait_recv()

    def part_copy(up, d, c):
        at = pl.ds(c * rows, rows)
        return pltpu.make_async_remote_copy(
            src_ref=part_ref.at[d, at], dst_ref=(up_ref if up else down_ref).at[d, at],
            send_sem=part_send.at[d, c], recv_sem=(up_recv if up else down_recv).at[d, c],
            device_id={"head": z + 1 if up else z - 1}, device_id_type=pl.DeviceIdType.MESH,
        )

    gain = gain_ref[...]
    for c in range(steps):
        at = slice(c * rows, (c + 1) * rows)
        for h in range(heads):
            cs = slice(h * DV, (h + 1) * DV)
            o = out_ref[at, cs] + mm(qeff_ref[at, cs], start_ref[h])
            n = o * lax.rsqrt(jnp.mean(o * o, -1, keepdims=True) + 1e-06)
            hid_ref[at, cs] = (n * gain * silu(gate_ref[at, cs].astype(F32))).astype(BF16)
        hidden = hid_ref[at, :]
        for d in range(n_head):
            part_ref[d, at, :] = mm(hidden, weight_ref[:, d * width : (d + 1) * width]).astype(BF16)

        @pl.when(z == 0)
        def _():
            for d in range(n_head - 1, 0, -1):
                part_copy(True, d, c).start()

        @pl.when(z == n_head - 1)
        def _():
            for d in range(n_head - 1):
                part_copy(False, d, c).start()

    def pass_on(up, d, c):
        inside = (z > 0) & (z < d) if up else (z < n_head - 1) & (z > d)

        @pl.when(inside)
        def _():
            part_copy(up, d, c).wait_recv()
            at = slice(c * rows, (c + 1) * rows)
            landed = (up_ref if up else down_ref)[d, at, :].astype(F32)
            part_ref[d, at, :] = (part_ref[d, at, :].astype(F32) + landed).astype(BF16)
            part_copy(up, d, c).start()

    for c in range(steps):
        for d in range(n_head - 1, 0, -1):
            pass_on(True, d, c)
            pass_on(False, n_head - 1 - d, c)
    for c in range(steps):
        at = slice(c * rows, (c + 1) * rows)
        for d in range(n_head):

            @pl.when(z == d)
            def _():
                total = part_ref[d, at, :].astype(F32)
                if d > 0:
                    part_copy(True, d, c).wait_recv()
                    total = total + up_ref[d, at, :].astype(F32)
                if d < n_head - 1:
                    part_copy(False, d, c).wait_recv()
                    total = total + down_ref[d, at, :].astype(F32)
                mixed_ref[at, :] = total.astype(BF16)

    for b in range(bits + 1):
        for i in range(own):
            state_copy(b, i).wait_send()
    for c in range(steps):
        for d in range(n_head):

            @pl.when(z != d)
            def _():
                part_copy(True, d, c).wait_send()


def body(
    query_raw, key_raw, value_raw, conv_query, conv_key, conv_value,
    decay_log, write_beta, gate_input, norm_gain, out_weight,
):
    tokens = query_raw.shape[0]
    heads = value_raw.shape[1] // DV
    ratio = value_raw.shape[1] // key_raw.shape[1]
    channels = query_raw.shape[1] + key_raw.shape[1] + value_raw.shape[1]
    n_ctx, n_head = lax.axis_size("ctx"), lax.axis_size("head")
    rim = lax.ppermute(
        jnp.concatenate([x[tokens - RIM :] for x in (query_raw, key_raw, value_raw)], 1),
        "ctx",
        [(i, i + 1) for i in range(n_ctx - 1)],
    )
    vmem = pl.BlockSpec(memory_space=pltpu.VMEM)
    out, qeff, trans = pl.pallas_call(
        local_kernel,
        out_shape=(
            jax.ShapeDtypeStruct((tokens, heads * DV), F32),
            jax.ShapeDtypeStruct((tokens, heads * DK), BF16),
            jax.ShapeDtypeStruct((heads, DK, DV + DK), BF16),
        ),
        in_specs=[vmem] * 9,
        out_specs=[vmem] * 3,
        scratch_shapes=[
            pltpu.VMEM((8, channels), F32),
            pltpu.VMEM((ratio * CHUNK, ratio * CHUNK), BF16),
            pltpu.VMEM((heads, DK, DV + DK), F32),
        ],
        compiler_params=pltpu.CompilerParams(vmem_limit_bytes=48 * 2**20),
        name="local",
    )(
        query_raw, key_raw, value_raw, rim, conv_query, conv_key, conv_value,
        decay_log, write_beta,
    )
    bits = n_ctx.bit_length() - 1
    assert n_ctx == 2**bits and bits > 1
    own = heads // 2
    steps = 4
    features = out_weight.shape[1] // n_head
    parts = pltpu.VMEM((n_head, tokens, features), BF16)
    state = pltpu.VMEM((own, DK, DV + DK), F32)
    return pl.pallas_call(
        functools.partial(finish_kernel, bits, n_head, steps),
        out_shape=jax.ShapeDtypeStruct((tokens, features), BF16),
        in_specs=[vmem] * 6,
        out_specs=vmem,
        scratch_shapes=[
            pltpu.VMEM((heads, DK, DV), BF16),
            pltpu.VMEM((tokens, heads * DV), BF16),
            state,
            state,
            state,
            pltpu.VMEM((bits, own, DK, DV + DK), BF16),
            pltpu.VMEM((bits, own, DK, DV + DK), BF16),
            pltpu.VMEM((own, DK, DV), BF16),
            pltpu.VMEM((own, DK, DV), BF16),
            pltpu.VMEM((own, DK, DV), BF16),
            parts,
            parts,
            parts,
            pltpu.SemaphoreType.DMA((bits + 1, own)),
            pltpu.SemaphoreType.DMA((bits + 1, own)),
            pltpu.SemaphoreType.DMA((n_head, steps)),
            pltpu.SemaphoreType.DMA((n_head, steps)),
            pltpu.SemaphoreType.DMA((n_head, steps)),
        ],
        compiler_params=pltpu.CompilerParams(
            vmem_limit_bytes=48 * 2**20, collective_id=0, has_side_effects=True
        ),
        name="finish",
    )(out, qeff, trans, gate_input, norm_gain.reshape(1, DV), out_weight)


def solution(mesh):
    return jax.shard_map(
        body,
        mesh=mesh,
        in_specs=(
            P("ctx", "head"), P("ctx", "head"), P("ctx", "head"),
            P(None, "head"), P(None, "head"), P(None, "head"),
            P("head", "ctx"), P("head", "ctx"), P("ctx", "head"),
            P(), P("head", None),
        ),
        out_specs=P("ctx", "head"),
        check_vma=False,
    )
```

```python
import functools

import jax
import jax.numpy as jnp
from jax import lax
from jax.experimental import pallas as pl
from jax.experimental.pallas import tpu as pltpu
from jax.sharding import PartitionSpec as P

DK = 128
DV = 128
CONV = 4
BLOCK = 64
CHUNK = 2 * BLOCK
RIM = 16
F32 = jnp.float32
BF16 = jnp.bfloat16


def mm(a, b):
    return jnp.dot(a.astype(BF16), b.astype(BF16), preferred_element_type=F32)


def mm_nt(a, b):
    return lax.dot_general(
        a.astype(BF16), b.astype(BF16), (((1,), (1,)), ((), ())), preferred_element_type=F32
    )


def silu(x):
    return x / (1.0 + jnp.exp(-x))


def iota(shape, dim):
    return lax.broadcasted_iota(jnp.int32, shape, dim)


def conv_part(tail, rows, taps):
    whole = jnp.concatenate([tail, rows], 0)
    first = 8 - (CONV - 1)
    total = taps[0:1] * whole[first : first + CHUNK]
    for j in range(1, CONV):
        total = total + taps[j : j + 1] * whole[first + j : first + j + CHUNK]
    return silu(total)


def unit(x, scale):
    return x * (lax.rsqrt(jnp.sum(x * x, -1, keepdims=True) + 1e-06) * scale)


def local_kernel(
    q_ref, k_ref, v_ref, rim_ref, cq_ref, ck_ref, cv_ref, dec_ref, beta_ref,
    out_ref, qeff_ref, trans_ref,
    tail_ref, bd_ref, st_ref,
):
    tokens = q_ref.shape[0]
    key_heads = q_ref.shape[1] // DK
    heads = v_ref.shape[1] // DV
    ratio = heads // key_heads
    width = ratio * CHUNK
    qc, kc = q_ref.shape[1], k_ref.shape[1]

    tail_ref[...] = rim_ref[...].astype(F32)[RIM - 8 :]
    bd_ref[...] = (
        iota((width, width), 0) // BLOCK == iota((width, width), 1) // BLOCK
    ).astype(F32).astype(BF16)
    for h in range(heads):
        st_ref[h] = jnp.concatenate(
            [jnp.zeros((DK, DV), F32), (iota((DK, DK), 0) == iota((DK, DK), 1)).astype(F32)], 1
        )

    def diag(value):
        return jnp.concatenate([value] * (width // BLOCK), 0) * bd_ref[...]

    def step(c, unused):
        at = pl.ds(pl.multiple_of(c * CHUNK, CHUNK), CHUNK)
        row = iota((BLOCK, width), 0)
        lane = iota((BLOCK, width), 1)
        col = lane % BLOCK
        half = iota((BLOCK, CHUNK), 1) < BLOCK
        row1, col1 = iota((BLOCK, CHUNK), 0), iota((BLOCK, CHUNK), 1) % BLOCK
        eye = (row == col).astype(F32)

        dec = dec_ref[:, at]
        beta = beta_ref[:, at]
        tri = (
            (iota((CHUNK, CHUNK), 0) <= iota((CHUNK, CHUNK), 1))
            & (iota((CHUNK, CHUNK), 0) // BLOCK == iota((CHUNK, CHUNK), 1) // BLOCK)
        ).astype(F32)
        cum = jnp.dot(dec, tri, precision=lax.Precision.HIGHEST, preferred_element_type=F32)
        last = jnp.where(
            iota((heads, CHUNK), 1) < BLOCK, cum[:, BLOCK - 1 : BLOCK], cum[:, CHUNK - 1 : CHUNK]
        )
        grow = jnp.exp(cum)
        rows = jnp.concatenate(
            [cum, beta, beta * grow, grow, jnp.exp(last - cum)], 0
        )
        cols = jnp.transpose(
            jnp.concatenate([rows, jnp.zeros((CHUNK - rows.shape[0], CHUNK), F32)], 0)
        )

        def column(kind, h):
            return cols[:, kind * heads + h : kind * heads + h + 1]

        def compact(x):
            return jnp.where(half, x[:BLOCK], x[BLOCK:])

        def conv(ref, taps_ref, offset, part):
            s = pl.ds(part * DK, DK)
            t = pl.ds(offset + part * DK, DK)
            new = ref[at, s].astype(F32)
            result = conv_part(tail_ref[:, t], new, taps_ref[:, s].astype(F32))
            tail_ref[:, t] = new[CHUNK - 8 :]
            return result

        queries, keys, lowers, scores, values = [], [], [], [], []
        for kh in range(key_heads):
            q = unit(conv(q_ref, cq_ref, 0, kh), DK ** (-0.5))
            k = unit(conv(k_ref, ck_ref, qc, kh), 1.0)
            kk = compact(mm_nt(k, k))
            qk = compact(mm_nt(q, k))
            low = []
            for g in range(ratio):
                h = kh * ratio + g
                values.append(conv(v_ref, cv_ref, qc + kc, h))
                cc = compact(jnp.broadcast_to(column(0, h), (CHUNK, CHUNK)))
                bc = compact(jnp.broadcast_to(column(1, h), (CHUNK, CHUNK)))
                spread = jnp.exp(jnp.where(row1 >= col1, cc - cum[h : h + 1], 0.0))
                low.append(jnp.where(row1 > col1, bc * kk * spread, 0.0))
                scores.append(jnp.where(row1 >= col1, qk * spread, 0.0).astype(BF16))
            lowers.append(jnp.concatenate(low, 1))
            queries.append(q)
            keys.append(k)

        inverse = [eye - jnp.where(row // 2 == col // 2, low, 0.0) for low in lowers]
        size = 2
        while size < BLOCK:
            off = (row // (2 * size) == col // (2 * size)) & (row // size > col // size)
            left = [
                mm(x, diag(jnp.where(off, low, 0.0).astype(BF16)))
                for x, low in zip(inverse, lowers)
            ]
            inverse = [x - mm(p, diag(x.astype(BF16))) for x, p in zip(inverse, left)]
            size *= 2

        mixes = []
        for kh in range(key_heads):
            rhs = []
            for g in range(ratio):
                h = kh * ratio + g
                rhs.append(
                    jnp.concatenate([column(2, h) * keys[kh], column(1, h) * values[h]], 1)
                )
            mixes.append(mm(diag(inverse[kh].astype(BF16)), jnp.concatenate(rhs, 0)))

        firsts, seconds = [], []
        for h in range(heads):
            kh, g = h // ratio, h % ratio
            firsts.append((column(3, h) * queries[kh]).astype(BF16))
            turned = jnp.transpose(column(4, h) * keys[kh]).astype(BF16)
            seconds.append(jnp.concatenate([scores[h], turned], 0))

        for s in range(CHUNK // BLOCK):
            one = []
            for h in range(heads):
                kh, g = h // ratio, h % ratio
                mix = mixes[kh][g * CHUNK + s * BLOCK : g * CHUNK + (s + 1) * BLOCK]
                lhs = jnp.concatenate(
                    [mix[:, :DK].astype(BF16), firsts[h][s * BLOCK : (s + 1) * BLOCK]], 0
                )
                one.append((mm(lhs, st_ref[h]), mix[:, DK:]))
            for h in range(heads):
                r1, u = one[h]
                fresh = jnp.concatenate([u - r1[:BLOCK, :DV], -r1[:BLOCK, DV:]], 1).astype(BF16)
                zero = jnp.zeros_like(fresh)
                r2 = mm(seconds[h], jnp.concatenate([fresh, zero] if s == 0 else [zero, fresh], 0))
                result = r1[BLOCK:] + r2[:BLOCK]
                where = pl.ds(pl.multiple_of(c * CHUNK + s * BLOCK, BLOCK), BLOCK)
                out_ref[where, h * DV : (h + 1) * DV] = result[:, :DV]
                qeff_ref[where, h * DK : (h + 1) * DK] = result[:, DV:].astype(BF16)
                decay = jnp.exp(cum[h : h + 1, (s + 1) * BLOCK - 1 : (s + 1) * BLOCK])
                st_ref[h] = decay * st_ref[h] + r2[BLOCK:]
        return unused

    lax.fori_loop(0, tokens // CHUNK, step, 0)
    trans_ref[...] = st_ref[...].astype(BF16)


def compose(later, earlier):
    moved = mm(later[:, DV:], earlier)
    return jnp.concatenate([moved[:, :DV] + later[:, :DV], moved[:, DV:]], 1)


def finish_kernel(
    bits, n_head, steps,
    out_ref, qeff_ref, trans_ref, gate_ref, gain_ref, weight_ref, mixed_ref,
    start_ref, hid_ref, total_ref, prefix_ref, low_ref, give_ref, got_ref, give_b_ref, got_b_ref,
    give_s_ref, part_ref, up_ref, down_ref,
    state_send, state_recv, part_send, up_recv, down_recv,
):
    heads = trans_ref.shape[0]
    own = heads // 2
    tokens = out_ref.shape[0]
    rows = tokens // steps
    width = mixed_ref.shape[1]
    me, z = lax.axis_index("ctx"), lax.axis_index("head")
    core = me % 2
    first, other = core * own, (1 - core) * own

    def bit(b):
        return (me // 2**b) % 2

    def partner(b):
        return {"ctx": me + (1 - 2 * bit(b)) * 2**b}

    barrier = pltpu.get_barrier_semaphore()
    for b in range(bits):
        pl.semaphore_signal(
            barrier, inc=1, device_id=partner(b), device_id_type=pl.DeviceIdType.MESH
        )

    @pl.when(z > 0)
    def _():
        pl.semaphore_signal(
            barrier, inc=1, device_id={"head": z - 1}, device_id_type=pl.DeviceIdType.MESH
        )

    @pl.when(z < n_head - 1)
    def _():
        pl.semaphore_signal(
            barrier, inc=1, device_id={"head": z + 1}, device_id_type=pl.DeviceIdType.MESH
        )

    inner = (z > 0) & (z < n_head - 1)

    @pl.when(inner)
    def _():
        pl.semaphore_wait(barrier, bits + 2)

    @pl.when(jnp.logical_not(inner))
    def _():
        pl.semaphore_wait(barrier, bits + 1)

    def state_copy(b, i):
        if b == 0:
            src, dst = trans_ref.at[other + i], got_ref.at[0, i]
        elif b == bits:
            src, dst = give_s_ref.at[i], start_ref.at[first + i]
        elif b == bits - 1:
            src, dst = give_b_ref.at[i], got_b_ref.at[i]
        else:
            src, dst = give_ref.at[b, i], got_ref.at[b, i]
        return pltpu.make_async_remote_copy(
            src_ref=src, dst_ref=dst, send_sem=state_send.at[b, i], recv_sem=state_recv.at[b, i],
            device_id=partner(0 if b == bits else b), device_id_type=pl.DeviceIdType.MESH,
        )

    for i in range(own):
        state_copy(0, i).start()
    fresh = jnp.concatenate(
        [jnp.zeros((DK, DV), F32), (iota((DK, DK), 0) == iota((DK, DK), 1)).astype(F32)], 1
    )
    for i in range(own):
        state_copy(0, i).wait_recv()
        mine = trans_ref[first + i].astype(F32)
        got = got_ref[0, i].astype(F32)
        low = jnp.where(core == 0, mine, got)
        total = compose(jnp.where(core == 0, got, mine), low)
        low_ref[i] = low
        total_ref[i] = total
        prefix_ref[i] = fresh
        if bits - 1 == 1:
            give_b_ref[i] = total[:, :DV].astype(BF16)
        else:
            give_ref[1, i] = total.astype(BF16)
        state_copy(1, i).start()
    for b in range(1, bits - 1):
        for i in range(own):
            state_copy(b, i).wait_recv()
            got = got_ref[b, i].astype(F32)
            total = total_ref[i]

            @pl.when(bit(b) == 1)
            def _():
                prefix_ref[i] = compose(prefix_ref[i], got)

            total = compose(
                jnp.where(bit(b) == 1, total, got), jnp.where(bit(b) == 1, got, total)
            )
            total_ref[i] = total
            if b + 1 == bits - 1:
                give_b_ref[i] = total[:, :DV].astype(BF16)
            else:
                give_ref[b + 1, i] = total.astype(BF16)
            state_copy(b + 1, i).start()
    for i in range(own):
        state_copy(bits - 1, i).wait_recv()
        prefix = prefix_ref[i]
        moved = mm(prefix[:, DV:], got_b_ref[i]) + prefix[:, :DV]
        chip = jnp.where(bit(bits - 1) == 1, moved, prefix[:, :DV])
        low = low_ref[i]
        later = mm(low[:, DV:], chip) + low[:, :DV]
        start_ref[first + i] = jnp.where(core == 0, chip, later).astype(BF16)
        give_s_ref[i] = jnp.where(core == 0, later, chip).astype(BF16)
        state_copy(bits, i).start()
    for i in range(own):
        pltpu.make_async_remote_copy(
            src_ref=give_s_ref.at[i], dst_ref=start_ref.at[other + i],
            send_sem=state_send.at[bits, i], recv_sem=state_recv.at[bits, i],
            device_id=partner(0), device_id_type=pl.DeviceIdType.MESH,
        ).wait_recv()

    def part_copy(up, d, c):
        at = pl.ds(c * rows, rows)
        return pltpu.make_async_remote_copy(
            src_ref=part_ref.at[d, at], dst_ref=(up_ref if up else down_ref).at[d, at],
            send_sem=part_send.at[d, c], recv_sem=(up_recv if up else down_recv).at[d, c],
            device_id={"head": z + 1 if up else z - 1}, device_id_type=pl.DeviceIdType.MESH,
        )

    gain = gain_ref[...]
    for c in range(steps):
        at = slice(c * rows, (c + 1) * rows)
        for h in range(heads):
            cs = slice(h * DV, (h + 1) * DV)
            o = out_ref[at, cs] + mm(qeff_ref[at, cs], start_ref[h])
            n = o * lax.rsqrt(jnp.mean(o * o, -1, keepdims=True) + 1e-06)
            hid_ref[at, cs] = (n * gain * silu(gate_ref[at, cs].astype(F32))).astype(BF16)
        hidden = hid_ref[at, :]
        for d in range(n_head):
            part_ref[d, at, :] = mm(hidden, weight_ref[:, d * width : (d + 1) * width]).astype(BF16)

        @pl.when(z == 0)
        def _():
            for d in range(n_head - 1, 0, -1):
                part_copy(True, d, c).start()

        @pl.when(z == n_head - 1)
        def _():
            for d in range(n_head - 1):
                part_copy(False, d, c).start()

    def pass_on(up, d, c):
        inside = (z > 0) & (z < d) if up else (z < n_head - 1) & (z > d)

        @pl.when(inside)
        def _():
            part_copy(up, d, c).wait_recv()
            at = slice(c * rows, (c + 1) * rows)
            landed = (up_ref if up else down_ref)[d, at, :].astype(F32)
            part_ref[d, at, :] = (part_ref[d, at, :].astype(F32) + landed).astype(BF16)
            part_copy(up, d, c).start()

    for c in range(steps):
        for d in range(n_head - 1, 0, -1):
            pass_on(True, d, c)
            pass_on(False, n_head - 1 - d, c)
    for c in range(steps):
        at = slice(c * rows, (c + 1) * rows)
        for d in range(n_head):

            @pl.when(z == d)
            def _():
                total = part_ref[d, at, :].astype(F32)
                if d > 0:
                    part_copy(True, d, c).wait_recv()
                    total = total + up_ref[d, at, :].astype(F32)
                if d < n_head - 1:
                    part_copy(False, d, c).wait_recv()
                    total = total + down_ref[d, at, :].astype(F32)
                mixed_ref[at, :] = total.astype(BF16)

    for b in range(bits + 1):
        for i in range(own):
            state_copy(b, i).wait_send()
    for c in range(steps):
        for d in range(n_head):

            @pl.when(z != d)
            def _():
                part_copy(True, d, c).wait_send()


def body(
    query_raw, key_raw, value_raw, conv_query, conv_key, conv_value,
    decay_log, write_beta, gate_input, norm_gain, out_weight,
):
    tokens = query_raw.shape[0]
    heads = value_raw.shape[1] // DV
    ratio = value_raw.shape[1] // key_raw.shape[1]
    channels = query_raw.shape[1] + key_raw.shape[1] + value_raw.shape[1]
    n_ctx, n_head = lax.axis_size("ctx"), lax.axis_size("head")
    rim = lax.ppermute(
        jnp.concatenate([x[tokens - RIM :] for x in (query_raw, key_raw, value_raw)], 1),
        "ctx",
        [(i, i + 1) for i in range(n_ctx - 1)],
    )
    vmem = pl.BlockSpec(memory_space=pltpu.VMEM)
    out, qeff, trans = pl.pallas_call(
        local_kernel,
        out_shape=(
            jax.ShapeDtypeStruct((tokens, heads * DV), F32),
            jax.ShapeDtypeStruct((tokens, heads * DK), BF16),
            jax.ShapeDtypeStruct((heads, DK, DV + DK), BF16),
        ),
        grid=(1,),
        in_specs=[
            pl.BlockSpec(x.shape, lambda i: (0, 0))
            for x in (
                query_raw, key_raw, value_raw, rim, conv_query, conv_key, conv_value,
                decay_log, write_beta,
            )
        ],
        out_specs=[vmem] * 3,
        scratch_shapes=[
            pltpu.VMEM((8, channels), F32),
            pltpu.VMEM((ratio * CHUNK, ratio * CHUNK), BF16),
            pltpu.VMEM((heads, DK, DV + DK), F32),
        ],
        compiler_params=pltpu.CompilerParams(vmem_limit_bytes=48 * 2**20),
        name="local",
    )(
        query_raw, key_raw, value_raw, rim, conv_query, conv_key, conv_value,
        decay_log, write_beta,
    )
    bits = n_ctx.bit_length() - 1
    assert n_ctx == 2**bits and bits > 1
    own = heads // 2
    steps = 4
    features = out_weight.shape[1] // n_head
    parts = pltpu.VMEM((n_head, tokens, features), BF16)
    state = pltpu.VMEM((own, DK, DV + DK), F32)
    return pl.pallas_call(
        functools.partial(finish_kernel, bits, n_head, steps),
        out_shape=jax.ShapeDtypeStruct((tokens, features), BF16),
        in_specs=[vmem] * 6,
        out_specs=vmem,
        scratch_shapes=[
            pltpu.VMEM((heads, DK, DV), BF16),
            pltpu.VMEM((tokens, heads * DV), BF16),
            state,
            state,
            state,
            pltpu.VMEM((bits, own, DK, DV + DK), BF16),
            pltpu.VMEM((bits, own, DK, DV + DK), BF16),
            pltpu.VMEM((own, DK, DV), BF16),
            pltpu.VMEM((own, DK, DV), BF16),
            pltpu.VMEM((own, DK, DV), BF16),
            parts,
            parts,
            parts,
            pltpu.SemaphoreType.DMA((bits + 1, own)),
            pltpu.SemaphoreType.DMA((bits + 1, own)),
            pltpu.SemaphoreType.DMA((n_head, steps)),
            pltpu.SemaphoreType.DMA((n_head, steps)),
            pltpu.SemaphoreType.DMA((n_head, steps)),
        ],
        compiler_params=pltpu.CompilerParams(
            vmem_limit_bytes=48 * 2**20, collective_id=0, has_side_effects=True
        ),
        name="finish",
    )(out, qeff, trans, gate_input, norm_gain.reshape(1, DV), out_weight)


def solution(mesh):
    return jax.shard_map(
        body,
        mesh=mesh,
        in_specs=(
            P("ctx", "head"), P("ctx", "head"), P("ctx", "head"),
            P(None, "head"), P(None, "head"), P(None, "head"),
            P("head", "ctx"), P("head", "ctx"), P("ctx", "head"),
            P(), P("head", None),
        ),
        out_specs=P("ctx", "head"),
        check_vma=False,
    )
```

```python
import functools

import jax
import jax.numpy as jnp
from jax import lax
from jax.experimental import pallas as pl
from jax.experimental.pallas import tpu as pltpu
from jax.sharding import PartitionSpec as P

DK = 128
DV = 128
CONV = 4
BLOCK = 64
CHUNK = 2 * BLOCK
RIM = 16
F32 = jnp.float32
BF16 = jnp.bfloat16


def mm(a, b):
    return jnp.dot(a.astype(BF16), b.astype(BF16), preferred_element_type=F32)


def mm_nt(a, b):
    return lax.dot_general(
        a.astype(BF16), b.astype(BF16), (((1,), (1,)), ((), ())), preferred_element_type=F32
    )


def silu(x):
    return x / (1.0 + jnp.exp(-x))


def iota(shape, dim):
    return lax.broadcasted_iota(jnp.int32, shape, dim)


def conv_part(tail, rows, taps):
    whole = jnp.concatenate([tail, rows], 0)
    first = 8 - (CONV - 1)
    total = taps[0:1] * whole[first : first + CHUNK]
    for j in range(1, CONV):
        total = total + taps[j : j + 1] * whole[first + j : first + j + CHUNK]
    return silu(total)


def unit(x, scale):
    return x * (lax.rsqrt(jnp.sum(x * x, -1, keepdims=True) + 1e-06) * scale)


def local_kernel(
    q_ref, k_ref, v_ref, rim_ref, cq_ref, ck_ref, cv_ref, dec_ref, beta_ref,
    out_ref, qeff_ref, trans_ref,
    tail_ref, bd_ref, st_ref,
):
    tokens = q_ref.shape[0]
    key_heads = q_ref.shape[1] // DK
    heads = v_ref.shape[1] // DV
    ratio = heads // key_heads
    width = ratio * CHUNK
    qc, kc = q_ref.shape[1], k_ref.shape[1]

    tail_ref[...] = rim_ref[...].astype(F32)[RIM - 8 :]
    bd_ref[...] = (
        iota((width, width), 0) // BLOCK == iota((width, width), 1) // BLOCK
    ).astype(F32).astype(BF16)
    for h in range(heads):
        st_ref[h] = jnp.concatenate(
            [jnp.zeros((DK, DV), F32), (iota((DK, DK), 0) == iota((DK, DK), 1)).astype(F32)], 1
        )

    def diag(value):
        return jnp.concatenate([value] * (width // BLOCK), 0) * bd_ref[...]

    def step(c, unused):
        at = pl.ds(pl.multiple_of(c * CHUNK, CHUNK), CHUNK)
        row = iota((BLOCK, width), 0)
        lane = iota((BLOCK, width), 1)
        col = lane % BLOCK
        half = iota((BLOCK, CHUNK), 1) < BLOCK
        row1, col1 = iota((BLOCK, CHUNK), 0), iota((BLOCK, CHUNK), 1) % BLOCK
        eye = (row == col).astype(F32)

        dec = dec_ref[:, at]
        beta = beta_ref[:, at]
        tri = (
            (iota((CHUNK, CHUNK), 0) <= iota((CHUNK, CHUNK), 1))
            & (iota((CHUNK, CHUNK), 0) // BLOCK == iota((CHUNK, CHUNK), 1) // BLOCK)
        ).astype(F32)
        cum = jnp.dot(dec, tri, precision=lax.Precision.HIGHEST, preferred_element_type=F32)
        last = jnp.where(
            iota((heads, CHUNK), 1) < BLOCK, cum[:, BLOCK - 1 : BLOCK], cum[:, CHUNK - 1 : CHUNK]
        )
        grow = jnp.exp(cum)
        rows = jnp.concatenate(
            [cum, beta, beta * grow, grow, jnp.exp(last - cum)], 0
        )
        cols = jnp.transpose(
            jnp.concatenate([rows, jnp.zeros((CHUNK - rows.shape[0], CHUNK), F32)], 0)
        )

        def column(kind, h):
            return cols[:, kind * heads + h : kind * heads + h + 1]

        def compact(x):
            return jnp.where(half, x[:BLOCK], x[BLOCK:])

        def conv(ref, taps_ref, offset, part):
            s = pl.ds(part * DK, DK)
            t = pl.ds(offset + part * DK, DK)
            new = ref[at, s].astype(F32)
            result = conv_part(tail_ref[:, t], new, taps_ref[:, s].astype(F32))
            tail_ref[:, t] = new[CHUNK - 8 :]
            return result

        queries, keys, lowers, scores, values = [], [], [], [], []
        for kh in range(key_heads):
            q = unit(conv(q_ref, cq_ref, 0, kh), DK ** (-0.5))
            k = unit(conv(k_ref, ck_ref, qc, kh), 1.0)
            kk = compact(mm_nt(k, k))
            qk = compact(mm_nt(q, k))
            low = []
            for g in range(ratio):
                h = kh * ratio + g
                values.append(conv(v_ref, cv_ref, qc + kc, h))
                cc = compact(jnp.broadcast_to(column(0, h), (CHUNK, CHUNK)))
                bc = compact(jnp.broadcast_to(column(1, h), (CHUNK, CHUNK)))
                spread = jnp.exp(jnp.where(row1 >= col1, cc - cum[h : h + 1], 0.0))
                low.append(jnp.where(row1 > col1, bc * kk * spread, 0.0))
                scores.append(jnp.where(row1 >= col1, qk * spread, 0.0).astype(BF16))
            lowers.append(jnp.concatenate(low, 1))
            queries.append(q)
            keys.append(k)

        inverse = [eye - jnp.where(row // 2 == col // 2, low, 0.0) for low in lowers]
        size = 2
        while size < BLOCK:
            off = (row // (2 * size) == col // (2 * size)) & (row // size > col // size)
            left = [
                mm(x, diag(jnp.where(off, low, 0.0).astype(BF16)))
                for x, low in zip(inverse, lowers)
            ]
            inverse = [x - mm(p, diag(x.astype(BF16))) for x, p in zip(inverse, left)]
            size *= 2

        mixes = []
        for kh in range(key_heads):
            rhs = []
            for g in range(ratio):
                h = kh * ratio + g
                rhs.append(
                    jnp.concatenate([column(2, h) * keys[kh], column(1, h) * values[h]], 1)
                )
            mixes.append(mm(diag(inverse[kh].astype(BF16)), jnp.concatenate(rhs, 0)))

        firsts, seconds = [], []
        for h in range(heads):
            kh, g = h // ratio, h % ratio
            firsts.append((column(3, h) * queries[kh]).astype(BF16))
            turned = jnp.transpose(column(4, h) * keys[kh]).astype(BF16)
            seconds.append(jnp.concatenate([scores[h], turned], 0))

        for s in range(CHUNK // BLOCK):
            one = []
            for h in range(heads):
                kh, g = h // ratio, h % ratio
                mix = mixes[kh][g * CHUNK + s * BLOCK : g * CHUNK + (s + 1) * BLOCK]
                lhs = jnp.concatenate(
                    [mix[:, :DK].astype(BF16), firsts[h][s * BLOCK : (s + 1) * BLOCK]], 0
                )
                one.append((mm(lhs, st_ref[h]), mix[:, DK:]))
            for h in range(heads):
                r1, u = one[h]
                fresh = jnp.concatenate([u - r1[:BLOCK, :DV], -r1[:BLOCK, DV:]], 1).astype(BF16)
                zero = jnp.zeros_like(fresh)
                r2 = mm(seconds[h], jnp.concatenate([fresh, zero] if s == 0 else [zero, fresh], 0))
                result = r1[BLOCK:] + r2[:BLOCK]
                where = pl.ds(pl.multiple_of(c * CHUNK + s * BLOCK, BLOCK), BLOCK)
                out_ref[where, h * DV : (h + 1) * DV] = result[:, :DV]
                qeff_ref[where, h * DK : (h + 1) * DK] = result[:, DV:].astype(BF16)
                decay = jnp.exp(cum[h : h + 1, (s + 1) * BLOCK - 1 : (s + 1) * BLOCK])
                st_ref[h] = decay * st_ref[h] + r2[BLOCK:]
        return unused

    lax.fori_loop(0, tokens // CHUNK, step, 0)
    trans_ref[...] = st_ref[...].astype(BF16)


def compose(later, earlier):
    moved = mm(later[:, DV:], earlier)
    return jnp.concatenate([moved[:, :DV] + later[:, :DV], moved[:, DV:]], 1)


def finish_kernel(
    bits, n_head, steps,
    out_ref, qeff_ref, trans_ref, gate_ref, gain_ref, weight_ref, mixed_ref,
    start_ref, hid_ref, total_ref, prefix_ref, low_ref, give_ref, got_ref, give_b_ref, got_b_ref,
    give_s_ref, part_ref, up_ref, down_ref,
    state_send, state_recv, part_send, up_recv, down_recv,
):
    heads = trans_ref.shape[0]
    own = heads // 2
    tokens = out_ref.shape[0]
    rows = tokens // steps
    group = 2
    width = mixed_ref.shape[1]
    me, z = lax.axis_index("ctx"), lax.axis_index("head")
    core = me % 2
    first, other = core * own, (1 - core) * own

    def bit(b):
        return (me // 2**b) % 2

    def partner(b):
        return {"ctx": me + (1 - 2 * bit(b)) * 2**b}

    barrier = pltpu.get_barrier_semaphore()
    for b in range(bits):
        pl.semaphore_signal(
            barrier, inc=1, device_id=partner(b), device_id_type=pl.DeviceIdType.MESH
        )

    @pl.when(z > 0)
    def _():
        pl.semaphore_signal(
            barrier, inc=1, device_id={"head": z - 1}, device_id_type=pl.DeviceIdType.MESH
        )

    @pl.when(z < n_head - 1)
    def _():
        pl.semaphore_signal(
            barrier, inc=1, device_id={"head": z + 1}, device_id_type=pl.DeviceIdType.MESH
        )

    inner = (z > 0) & (z < n_head - 1)

    @pl.when(inner)
    def _():
        pl.semaphore_wait(barrier, bits + 2)

    @pl.when(jnp.logical_not(inner))
    def _():
        pl.semaphore_wait(barrier, bits + 1)

    def state_copy(b, i):
        if b == 0:
            src, dst = trans_ref.at[other + i], got_ref.at[0, i]
        elif b == bits:
            src, dst = give_s_ref.at[i], start_ref.at[first + i]
        elif b == bits - 1:
            src, dst = give_b_ref.at[i], got_b_ref.at[i]
        else:
            src, dst = give_ref.at[b, i], got_ref.at[b, i]
        return pltpu.make_async_remote_copy(
            src_ref=src, dst_ref=dst, send_sem=state_send.at[b, i], recv_sem=state_recv.at[b, i],
            device_id=partner(0 if b == bits else b), device_id_type=pl.DeviceIdType.MESH,
        )

    for i in range(own):
        state_copy(0, i).start()
    fresh = jnp.concatenate(
        [jnp.zeros((DK, DV), F32), (iota((DK, DK), 0) == iota((DK, DK), 1)).astype(F32)], 1
    )
    for i in range(own):
        state_copy(0, i).wait_recv()
        mine = trans_ref[first + i].astype(F32)
        got = got_ref[0, i].astype(F32)
        low = jnp.where(core == 0, mine, got)
        total = compose(jnp.where(core == 0, got, mine), low)
        low_ref[i] = low
        total_ref[i] = total
        prefix_ref[i] = fresh
        if bits - 1 == 1:
            give_b_ref[i] = total[:, :DV].astype(BF16)
        else:
            give_ref[1, i] = total.astype(BF16)
        state_copy(1, i).start()
    for b in range(1, bits - 1):
        for i in range(own):
            state_copy(b, i).wait_recv()
            got = got_ref[b, i].astype(F32)
            total = total_ref[i]

            @pl.when(bit(b) == 1)
            def _():
                prefix_ref[i] = compose(prefix_ref[i], got)

            total = compose(
                jnp.where(bit(b) == 1, total, got), jnp.where(bit(b) == 1, got, total)
            )
            total_ref[i] = total
            if b + 1 == bits - 1:
                give_b_ref[i] = total[:, :DV].astype(BF16)
            else:
                give_ref[b + 1, i] = total.astype(BF16)
            state_copy(b + 1, i).start()
    for i in range(own):
        state_copy(bits - 1, i).wait_recv()
        prefix = prefix_ref[i]
        moved = mm(prefix[:, DV:], got_b_ref[i]) + prefix[:, :DV]
        chip = jnp.where(bit(bits - 1) == 1, moved, prefix[:, :DV])
        low = low_ref[i]
        later = mm(low[:, DV:], chip) + low[:, :DV]
        start_ref[first + i] = jnp.where(core == 0, chip, later).astype(BF16)
        give_s_ref[i] = jnp.where(core == 0, later, chip).astype(BF16)
        state_copy(bits, i).start()
    for i in range(own):
        pltpu.make_async_remote_copy(
            src_ref=give_s_ref.at[i], dst_ref=start_ref.at[other + i],
            send_sem=state_send.at[bits, i], recv_sem=state_recv.at[bits, i],
            device_id=partner(0), device_id_type=pl.DeviceIdType.MESH,
        ).wait_recv()

    def piece(c):
        return pl.ds(pl.multiple_of(c * rows, rows), rows)

    def part_copy(up, d, c):
        at = piece(c)
        return pltpu.make_async_remote_copy(
            src_ref=part_ref.at[d, at], dst_ref=(up_ref if up else down_ref).at[d, at],
            send_sem=part_send.at[d, c], recv_sem=(up_recv if up else down_recv).at[d, c],
            device_id={"head": z + 1 if up else z - 1}, device_id_type=pl.DeviceIdType.MESH,
        )

    gain = gain_ref[...]
    for t in range(steps // group):
        at = slice(t * group * rows, (t + 1) * group * rows)
        for h in range(heads):
            cs = slice(h * DV, (h + 1) * DV)
            o = out_ref[at, cs] + mm(qeff_ref[at, cs], start_ref[h])
            n = o * lax.rsqrt(jnp.mean(o * o, -1, keepdims=True) + 1e-06)
            hid_ref[at, cs] = (n * gain * silu(gate_ref[at, cs].astype(F32))).astype(BF16)
        hidden = hid_ref[at, :]
        for d in range(n_head):
            part_ref[d, at, :] = mm(hidden, weight_ref[:, d * width : (d + 1) * width]).astype(BF16)

        def feed(up, targets):
            for c in range(t * group, (t + 1) * group):
                for d in targets:
                    if c > 0:
                        part_copy(up, d, c - 1).wait_send()
                    part_copy(up, d, c).start()

        @pl.when(z == 0)
        def _():
            feed(True, range(n_head - 1, 0, -1))

        @pl.when(z == n_head - 1)
        def _():
            feed(False, range(n_head - 1))

    def pass_on(up, d, c):
        inside = (z > 0) & (z < d) if up else (z < n_head - 1) & (z > d)

        @pl.when(inside)
        def _():
            part_copy(up, d, c).wait_recv()
            landed = (up_ref if up else down_ref)[d, piece(c), :].astype(F32)
            part_ref[d, piece(c), :] = (part_ref[d, piece(c), :].astype(F32) + landed).astype(BF16)
            part_copy(up, d, c).start()

    def ups(c):
        for d in range(n_head - 1, 0, -1):
            pass_on(True, d, c)

    def downs(c):
        for d in range(n_head - 1):
            pass_on(False, d, c)

    @pl.when(z < n_head // 2)
    def _():
        def lap(c, unused):
            ups(c)
            downs(c)
            return unused

        lax.fori_loop(0, steps, lap, 0)

    @pl.when(z >= n_head // 2)
    def _():
        def lap(c, unused):
            downs(c)
            ups(c)
            return unused

        lax.fori_loop(0, steps, lap, 0)

    def close(c, unused):
        for d in range(n_head):

            @pl.when(z == d)
            def _():
                total = part_ref[d, piece(c), :].astype(F32)
                if d > 0:
                    part_copy(True, d, c).wait_recv()
                    total = total + up_ref[d, piece(c), :].astype(F32)
                if d < n_head - 1:
                    part_copy(False, d, c).wait_recv()
                    total = total + down_ref[d, piece(c), :].astype(F32)
                mixed_ref[piece(c), :] = total.astype(BF16)

        return unused

    lax.fori_loop(0, steps, close, 0)

    for b in range(bits + 1):
        for i in range(own):
            state_copy(b, i).wait_send()
    for c in range(steps):
        for d in range(n_head):
            unsent = z != d
            if c < steps - 1:
                unsent = unsent & (z > 0) & (z < n_head - 1)

            @pl.when(unsent)
            def _():
                part_copy(True, d, c).wait_send()


def body(
    query_raw, key_raw, value_raw, conv_query, conv_key, conv_value,
    decay_log, write_beta, gate_input, norm_gain, out_weight,
):
    tokens = query_raw.shape[0]
    heads = value_raw.shape[1] // DV
    ratio = value_raw.shape[1] // key_raw.shape[1]
    channels = query_raw.shape[1] + key_raw.shape[1] + value_raw.shape[1]
    n_ctx, n_head = lax.axis_size("ctx"), lax.axis_size("head")
    rim = lax.ppermute(
        jnp.concatenate([x[tokens - RIM :] for x in (query_raw, key_raw, value_raw)], 1),
        "ctx",
        [(i, i + 1) for i in range(n_ctx - 1)],
    )
    vmem = pl.BlockSpec(memory_space=pltpu.VMEM)
    out, qeff, trans = pl.pallas_call(
        local_kernel,
        out_shape=(
            jax.ShapeDtypeStruct((tokens, heads * DV), F32),
            jax.ShapeDtypeStruct((tokens, heads * DK), BF16),
            jax.ShapeDtypeStruct((heads, DK, DV + DK), BF16),
        ),
        grid=(1,),
        in_specs=[
            pl.BlockSpec(x.shape, lambda i: (0, 0))
            for x in (
                query_raw, key_raw, value_raw, rim, conv_query, conv_key, conv_value,
                decay_log, write_beta,
            )
        ],
        out_specs=[vmem] * 3,
        scratch_shapes=[
            pltpu.VMEM((8, channels), F32),
            pltpu.VMEM((ratio * CHUNK, ratio * CHUNK), BF16),
            pltpu.VMEM((heads, DK, DV + DK), F32),
        ],
        compiler_params=pltpu.CompilerParams(vmem_limit_bytes=48 * 2**20),
        name="local",
    )(
        query_raw, key_raw, value_raw, rim, conv_query, conv_key, conv_value,
        decay_log, write_beta,
    )
    bits = n_ctx.bit_length() - 1
    assert n_ctx == 2**bits and bits > 1
    own = heads // 2
    steps = 8
    features = out_weight.shape[1] // n_head
    parts = pltpu.VMEM((n_head, tokens, features), BF16)
    state = pltpu.VMEM((own, DK, DV + DK), F32)
    return pl.pallas_call(
        functools.partial(finish_kernel, bits, n_head, steps),
        out_shape=jax.ShapeDtypeStruct((tokens, features), BF16),
        in_specs=[vmem] * 6,
        out_specs=vmem,
        scratch_shapes=[
            pltpu.VMEM((heads, DK, DV), BF16),
            pltpu.VMEM((tokens, heads * DV), BF16),
            state,
            state,
            state,
            pltpu.VMEM((bits, own, DK, DV + DK), BF16),
            pltpu.VMEM((bits, own, DK, DV + DK), BF16),
            pltpu.VMEM((own, DK, DV), BF16),
            pltpu.VMEM((own, DK, DV), BF16),
            pltpu.VMEM((own, DK, DV), BF16),
            parts,
            parts,
            parts,
            pltpu.SemaphoreType.DMA((bits + 1, own)),
            pltpu.SemaphoreType.DMA((bits + 1, own)),
            pltpu.SemaphoreType.DMA((n_head, steps)),
            pltpu.SemaphoreType.DMA((n_head, steps)),
            pltpu.SemaphoreType.DMA((n_head, steps)),
        ],
        compiler_params=pltpu.CompilerParams(
            vmem_limit_bytes=48 * 2**20, collective_id=0, has_side_effects=True
        ),
        name="finish",
    )(out, qeff, trans, gate_input, norm_gain.reshape(1, DV), out_weight)


def solution(mesh):
    return jax.shard_map(
        body,
        mesh=mesh,
        in_specs=(
            P("ctx", "head"), P("ctx", "head"), P("ctx", "head"),
            P(None, "head"), P(None, "head"), P(None, "head"),
            P("head", "ctx"), P("head", "ctx"), P("ctx", "head"),
            P(), P("head", None),
        ),
        out_specs=P("ctx", "head"),
        check_vma=False,
    )
```

```python
import functools

import jax
import jax.numpy as jnp
from jax import lax
from jax.experimental import pallas as pl
from jax.experimental.pallas import tpu as pltpu
from jax.sharding import PartitionSpec as P

DK = 128
DV = 128
CONV = 4
BLOCK = 64
CHUNK = 2 * BLOCK
RIM = 16
F32 = jnp.float32
BF16 = jnp.bfloat16


def mm(a, b):
    return jnp.dot(a.astype(BF16), b.astype(BF16), preferred_element_type=F32)


def mm_nt(a, b):
    return lax.dot_general(
        a.astype(BF16), b.astype(BF16), (((1,), (1,)), ((), ())), preferred_element_type=F32
    )


def silu(x):
    return x / (1.0 + jnp.exp(-x))


def iota(shape, dim):
    return lax.broadcasted_iota(jnp.int32, shape, dim)


def conv_part(tail, rows, taps):
    whole = jnp.concatenate([tail, rows], 0)
    first = 8 - (CONV - 1)
    total = taps[0:1] * whole[first : first + CHUNK]
    for j in range(1, CONV):
        total = total + taps[j : j + 1] * whole[first + j : first + j + CHUNK]
    return silu(total)


def unit(x, scale):
    return x * (lax.rsqrt(jnp.sum(x * x, -1, keepdims=True) + 1e-06) * scale)


def local_kernel(
    q_ref, k_ref, v_ref, rim_ref, cq_ref, ck_ref, cv_ref, dec_ref, beta_ref,
    out_ref, qeff_ref, trans_ref,
    tail_ref, bd_ref, st_ref,
):
    tokens = q_ref.shape[0]
    key_heads = q_ref.shape[1] // DK
    heads = v_ref.shape[1] // DV
    ratio = heads // key_heads
    width = ratio * CHUNK
    qc, kc = q_ref.shape[1], k_ref.shape[1]

    tail_ref[...] = rim_ref[...].astype(F32)[RIM - 8 :]
    bd_ref[...] = (
        iota((width, width), 0) // BLOCK == iota((width, width), 1) // BLOCK
    ).astype(F32).astype(BF16)
    for h in range(heads):
        st_ref[h] = jnp.concatenate(
            [jnp.zeros((DK, DV), F32), (iota((DK, DK), 0) == iota((DK, DK), 1)).astype(F32)], 1
        )

    def diag(value):
        return jnp.concatenate([value] * (width // BLOCK), 0) * bd_ref[...]

    def step(c, unused):
        at = pl.ds(pl.multiple_of(c * CHUNK, CHUNK), CHUNK)
        row = iota((BLOCK, width), 0)
        lane = iota((BLOCK, width), 1)
        col = lane % BLOCK
        half = iota((BLOCK, CHUNK), 1) < BLOCK
        row1, col1 = iota((BLOCK, CHUNK), 0), iota((BLOCK, CHUNK), 1) % BLOCK
        eye = (row == col).astype(F32)

        dec = dec_ref[:, at]
        beta = beta_ref[:, at]
        tri = (
            (iota((CHUNK, CHUNK), 0) <= iota((CHUNK, CHUNK), 1))
            & (iota((CHUNK, CHUNK), 0) // BLOCK == iota((CHUNK, CHUNK), 1) // BLOCK)
        ).astype(F32)
        cum = jnp.dot(dec, tri, precision=lax.Precision.HIGHEST, preferred_element_type=F32)
        last = jnp.where(
            iota((heads, CHUNK), 1) < BLOCK, cum[:, BLOCK - 1 : BLOCK], cum[:, CHUNK - 1 : CHUNK]
        )
        grow = jnp.exp(cum)
        rows = jnp.concatenate(
            [cum, beta, beta * grow, grow, jnp.exp(last - cum)], 0
        )
        cols = jnp.transpose(
            jnp.concatenate([rows, jnp.zeros((CHUNK - rows.shape[0], CHUNK), F32)], 0)
        )

        def column(kind, h):
            return cols[:, kind * heads + h : kind * heads + h + 1]

        def compact(x):
            return jnp.where(half, x[:BLOCK], x[BLOCK:])

        def conv(ref, taps_ref, offset, part):
            s = pl.ds(part * DK, DK)
            t = pl.ds(offset + part * DK, DK)
            new = ref[at, s].astype(F32)
            result = conv_part(tail_ref[:, t], new, taps_ref[:, s].astype(F32))
            tail_ref[:, t] = new[CHUNK - 8 :]
            return result

        queries, keys, lowers, scores, values = [], [], [], [], []
        for kh in range(key_heads):
            q = unit(conv(q_ref, cq_ref, 0, kh), DK ** (-0.5))
            k = unit(conv(k_ref, ck_ref, qc, kh), 1.0)
            kk = compact(mm_nt(k, k))
            qk = compact(mm_nt(q, k))
            low = []
            for g in range(ratio):
                h = kh * ratio + g
                values.append(conv(v_ref, cv_ref, qc + kc, h))
                cc = compact(jnp.broadcast_to(column(0, h), (CHUNK, CHUNK)))
                bc = compact(jnp.broadcast_to(column(1, h), (CHUNK, CHUNK)))
                spread = jnp.exp(jnp.where(row1 >= col1, cc - cum[h : h + 1], 0.0))
                low.append(jnp.where(row1 > col1, bc * kk * spread, 0.0))
                scores.append(jnp.where(row1 >= col1, qk * spread, 0.0).astype(BF16))
            lowers.append(jnp.concatenate(low, 1))
            queries.append(q)
            keys.append(k)

        inverse = [eye - jnp.where(row // 2 == col // 2, low, 0.0) for low in lowers]
        size = 2
        while size < BLOCK:
            off = (row // (2 * size) == col // (2 * size)) & (row // size > col // size)
            left = [
                mm(x, diag(jnp.where(off, low, 0.0).astype(BF16)))
                for x, low in zip(inverse, lowers)
            ]
            inverse = [x - mm(p, diag(x.astype(BF16))) for x, p in zip(inverse, left)]
            size *= 2

        mixes = []
        for kh in range(key_heads):
            rhs = []
            for g in range(ratio):
                h = kh * ratio + g
                rhs.append(
                    jnp.concatenate([column(2, h) * keys[kh], column(1, h) * values[h]], 1)
                )
            mixes.append(mm(diag(inverse[kh].astype(BF16)), jnp.concatenate(rhs, 0)))

        firsts, seconds = [], []
        for h in range(heads):
            kh, g = h // ratio, h % ratio
            firsts.append((column(3, h) * queries[kh]).astype(BF16))
            turned = jnp.transpose(column(4, h) * keys[kh]).astype(BF16)
            seconds.append(jnp.concatenate([scores[h], turned], 0))

        for s in range(CHUNK // BLOCK):
            one = []
            for h in range(heads):
                kh, g = h // ratio, h % ratio
                mix = mixes[kh][g * CHUNK + s * BLOCK : g * CHUNK + (s + 1) * BLOCK]
                lhs = jnp.concatenate(
                    [mix[:, :DK].astype(BF16), firsts[h][s * BLOCK : (s + 1) * BLOCK]], 0
                )
                one.append((mm(lhs, st_ref[h]), mix[:, DK:]))
            for h in range(heads):
                r1, u = one[h]
                fresh = jnp.concatenate([u - r1[:BLOCK, :DV], -r1[:BLOCK, DV:]], 1).astype(BF16)
                zero = jnp.zeros_like(fresh)
                r2 = mm(seconds[h], jnp.concatenate([fresh, zero] if s == 0 else [zero, fresh], 0))
                result = r1[BLOCK:] + r2[:BLOCK]
                where = pl.ds(pl.multiple_of(c * CHUNK + s * BLOCK, BLOCK), BLOCK)
                out_ref[where, h * DV : (h + 1) * DV] = result[:, :DV]
                qeff_ref[where, h * DK : (h + 1) * DK] = result[:, DV:].astype(BF16)
                decay = jnp.exp(cum[h : h + 1, (s + 1) * BLOCK - 1 : (s + 1) * BLOCK])
                st_ref[h] = decay * st_ref[h] + r2[BLOCK:]
        return unused

    lax.fori_loop(0, tokens // CHUNK, step, 0)
    trans_ref[...] = st_ref[...].astype(BF16)


def local_entry(
    q_ref, k_ref, v_ref, dec_ref, beta_ref, rim_ref, taps_ref,
    out_ref, qeff_ref, trans_ref,
    tail_ref, bd_ref, st_ref, q_in, k_in, v_in, dec_in, beta_in, sem,
):
    pairs = ((q_ref, q_in), (k_ref, k_in), (v_ref, v_in), (dec_ref, dec_in), (beta_ref, beta_in))
    copies = [pltpu.make_async_copy(a, b, sem.at[i]) for i, (a, b) in enumerate(pairs)]
    for copy in copies:
        copy.start()
    for copy in copies:
        copy.wait()
    qc, kc = q_ref.shape[1], k_ref.shape[1]
    local_kernel(
        q_in, k_in, v_in, rim_ref,
        taps_ref.at[:, :qc], taps_ref.at[:, qc : qc + kc], taps_ref.at[:, qc + kc :],
        dec_in, beta_in, out_ref, qeff_ref, trans_ref, tail_ref, bd_ref, st_ref,
    )


def compose(later, earlier):
    moved = mm(later[:, DV:], earlier)
    return jnp.concatenate([moved[:, :DV] + later[:, :DV], moved[:, DV:]], 1)


def finish_kernel(
    bits, n_head, steps,
    out_ref, qeff_ref, trans_ref, gate_hbm, gain_ref, weight_hbm, mixed_ref,
    start_ref, hid_ref, total_ref, prefix_ref, low_ref, give_ref, got_ref, give_b_ref, got_b_ref,
    give_s_ref, part_ref, up_ref, down_ref,
    state_send, state_recv, part_send, up_recv, down_recv,
    gate_ref, weight_ref, in_sem,
):
    heads = trans_ref.shape[0]
    own = heads // 2
    tokens = out_ref.shape[0]
    rows = tokens // steps
    group = 2
    width = mixed_ref.shape[1]
    me, z = lax.axis_index("ctx"), lax.axis_index("head")
    core = me % 2
    first, other = core * own, (1 - core) * own

    def bit(b):
        return (me // 2**b) % 2

    def partner(b):
        return {"ctx": me + (1 - 2 * bit(b)) * 2**b}

    gate_copy = pltpu.make_async_copy(gate_hbm, gate_ref, in_sem.at[0])
    weight_copy = pltpu.make_async_copy(weight_hbm, weight_ref, in_sem.at[1])
    gate_copy.start()
    weight_copy.start()
    barrier = pltpu.get_barrier_semaphore()
    for b in range(bits):
        pl.semaphore_signal(
            barrier, inc=1, device_id=partner(b), device_id_type=pl.DeviceIdType.MESH
        )

    @pl.when(z > 0)
    def _():
        pl.semaphore_signal(
            barrier, inc=1, device_id={"head": z - 1}, device_id_type=pl.DeviceIdType.MESH
        )

    @pl.when(z < n_head - 1)
    def _():
        pl.semaphore_signal(
            barrier, inc=1, device_id={"head": z + 1}, device_id_type=pl.DeviceIdType.MESH
        )

    inner = (z > 0) & (z < n_head - 1)

    @pl.when(inner)
    def _():
        pl.semaphore_wait(barrier, bits + 2)

    @pl.when(jnp.logical_not(inner))
    def _():
        pl.semaphore_wait(barrier, bits + 1)

    def state_copy(b, i):
        if b == 0:
            src, dst = trans_ref.at[other + i], got_ref.at[0, i]
        elif b == bits:
            src, dst = give_s_ref.at[i], start_ref.at[first + i]
        elif b == bits - 1:
            src, dst = give_b_ref.at[i], got_b_ref.at[i]
        else:
            src, dst = give_ref.at[b, i], got_ref.at[b, i]
        return pltpu.make_async_remote_copy(
            src_ref=src, dst_ref=dst, send_sem=state_send.at[b, i], recv_sem=state_recv.at[b, i],
            device_id=partner(0 if b == bits else b), device_id_type=pl.DeviceIdType.MESH,
        )

    for i in range(own):
        state_copy(0, i).start()
    fresh = jnp.concatenate(
        [jnp.zeros((DK, DV), F32), (iota((DK, DK), 0) == iota((DK, DK), 1)).astype(F32)], 1
    )
    for i in range(own):
        state_copy(0, i).wait_recv()
        mine = trans_ref[first + i].astype(F32)
        got = got_ref[0, i].astype(F32)
        low = jnp.where(core == 0, mine, got)
        total = compose(jnp.where(core == 0, got, mine), low)
        low_ref[i] = low
        total_ref[i] = total
        prefix_ref[i] = fresh
        if bits - 1 == 1:
            give_b_ref[i] = total[:, :DV].astype(BF16)
        else:
            give_ref[1, i] = total.astype(BF16)
        state_copy(1, i).start()
    for b in range(1, bits - 1):
        for i in range(own):
            state_copy(b, i).wait_recv()
            got = got_ref[b, i].astype(F32)
            total = total_ref[i]

            @pl.when(bit(b) == 1)
            def _():
                prefix_ref[i] = compose(prefix_ref[i], got)

            total = compose(
                jnp.where(bit(b) == 1, total, got), jnp.where(bit(b) == 1, got, total)
            )
            total_ref[i] = total
            if b + 1 == bits - 1:
                give_b_ref[i] = total[:, :DV].astype(BF16)
            else:
                give_ref[b + 1, i] = total.astype(BF16)
            state_copy(b + 1, i).start()
    for i in range(own):
        state_copy(bits - 1, i).wait_recv()
        prefix = prefix_ref[i]
        moved = mm(prefix[:, DV:], got_b_ref[i]) + prefix[:, :DV]
        chip = jnp.where(bit(bits - 1) == 1, moved, prefix[:, :DV])
        low = low_ref[i]
        later = mm(low[:, DV:], chip) + low[:, :DV]
        start_ref[first + i] = jnp.where(core == 0, chip, later).astype(BF16)
        give_s_ref[i] = jnp.where(core == 0, later, chip).astype(BF16)
        state_copy(bits, i).start()
    for i in range(own):
        pltpu.make_async_remote_copy(
            src_ref=give_s_ref.at[i], dst_ref=start_ref.at[other + i],
            send_sem=state_send.at[bits, i], recv_sem=state_recv.at[bits, i],
            device_id=partner(0), device_id_type=pl.DeviceIdType.MESH,
        ).wait_recv()

    def piece(c):
        return pl.ds(pl.multiple_of(c * rows, rows), rows)

    def part_copy(up, d, c):
        at = piece(c)
        return pltpu.make_async_remote_copy(
            src_ref=part_ref.at[d, at], dst_ref=(up_ref if up else down_ref).at[d, at],
            send_sem=part_send.at[d, c], recv_sem=(up_recv if up else down_recv).at[d, c],
            device_id={"head": z + 1 if up else z - 1}, device_id_type=pl.DeviceIdType.MESH,
        )

    gain = gain_ref[...]
    gate_copy.wait()
    weight_copy.wait()
    for t in range(steps // group):
        at = slice(t * group * rows, (t + 1) * group * rows)
        for h in range(heads):
            cs = slice(h * DV, (h + 1) * DV)
            o = out_ref[at, cs] + mm(qeff_ref[at, cs], start_ref[h])
            n = o * lax.rsqrt(jnp.mean(o * o, -1, keepdims=True) + 1e-06)
            hid_ref[at, cs] = (n * gain * silu(gate_ref[at, cs].astype(F32))).astype(BF16)
        hidden = hid_ref[at, :]
        for d in range(n_head):
            part_ref[d, at, :] = mm(hidden, weight_ref[:, d * width : (d + 1) * width]).astype(BF16)

        def feed(up, targets):
            for c in range(t * group, (t + 1) * group):
                for d in targets:
                    if c > 0:
                        part_copy(up, d, c - 1).wait_send()
                    part_copy(up, d, c).start()

        @pl.when(z == 0)
        def _():
            feed(True, range(n_head - 1, 0, -1))

        @pl.when(z == n_head - 1)
        def _():
            feed(False, range(n_head - 1))

    def pass_on(up, d, c):
        inside = (z > 0) & (z < d) if up else (z < n_head - 1) & (z > d)

        @pl.when(inside)
        def _():
            part_copy(up, d, c).wait_recv()
            landed = (up_ref if up else down_ref)[d, piece(c), :].astype(F32)
            part_ref[d, piece(c), :] = (part_ref[d, piece(c), :].astype(F32) + landed).astype(BF16)
            part_copy(up, d, c).start()

    def ups(c):
        for d in range(n_head - 1, 0, -1):
            pass_on(True, d, c)

    def downs(c):
        for d in range(n_head - 1):
            pass_on(False, d, c)

    @pl.when(z < n_head // 2)
    def _():
        def lap(c, unused):
            ups(c)
            downs(c)
            return unused

        lax.fori_loop(0, steps, lap, 0)

    @pl.when(z >= n_head // 2)
    def _():
        def lap(c, unused):
            downs(c)
            ups(c)
            return unused

        lax.fori_loop(0, steps, lap, 0)

    def close(c, unused):
        for d in range(n_head):

            @pl.when(z == d)
            def _():
                total = part_ref[d, piece(c), :].astype(F32)
                if d > 0:
                    part_copy(True, d, c).wait_recv()
                    total = total + up_ref[d, piece(c), :].astype(F32)
                if d < n_head - 1:
                    part_copy(False, d, c).wait_recv()
                    total = total + down_ref[d, piece(c), :].astype(F32)
                mixed_ref[piece(c), :] = total.astype(BF16)

        return unused

    lax.fori_loop(0, steps, close, 0)

    for b in range(bits + 1):
        for i in range(own):
            state_copy(b, i).wait_send()
    for c in range(steps):
        for d in range(n_head):
            unsent = z != d
            if c < steps - 1:
                unsent = unsent & (z > 0) & (z < n_head - 1)

            @pl.when(unsent)
            def _():
                part_copy(True, d, c).wait_send()


def body(
    query_raw, key_raw, value_raw, conv_query, conv_key, conv_value,
    decay_log, write_beta, gate_input, norm_gain, out_weight,
):
    tokens = query_raw.shape[0]
    heads = value_raw.shape[1] // DV
    ratio = value_raw.shape[1] // key_raw.shape[1]
    channels = query_raw.shape[1] + key_raw.shape[1] + value_raw.shape[1]
    n_ctx, n_head = lax.axis_size("ctx"), lax.axis_size("head")
    rim = lax.ppermute(
        jnp.concatenate([x[tokens - RIM :] for x in (query_raw, key_raw, value_raw)], 1),
        "ctx",
        [(i, i + 1) for i in range(n_ctx - 1)],
    )
    vmem = pl.BlockSpec(memory_space=pltpu.VMEM)
    hbm = pl.BlockSpec(memory_space=pltpu.HBM)
    out, qeff, trans = pl.pallas_call(
        local_entry,
        out_shape=(
            jax.ShapeDtypeStruct((tokens, heads * DV), F32),
            jax.ShapeDtypeStruct((tokens, heads * DK), BF16),
            jax.ShapeDtypeStruct((heads, DK, DV + DK), BF16),
        ),
        in_specs=[hbm] * 5 + [vmem] * 2,
        out_specs=[vmem] * 3,
        scratch_shapes=[
            pltpu.VMEM((8, channels), F32),
            pltpu.VMEM((ratio * CHUNK, ratio * CHUNK), BF16),
            pltpu.VMEM((heads, DK, DV + DK), F32),
            *(
                pltpu.VMEM(x.shape, x.dtype)
                for x in (query_raw, key_raw, value_raw, decay_log, write_beta)
            ),
            pltpu.SemaphoreType.DMA((5,)),
        ],
        compiler_params=pltpu.CompilerParams(vmem_limit_bytes=48 * 2**20),
        name="local",
    )(
        query_raw, key_raw, value_raw, decay_log, write_beta, rim,
        jnp.concatenate([conv_query, conv_key, conv_value], 1).astype(F32),
    )
    bits = n_ctx.bit_length() - 1
    assert n_ctx == 2**bits and bits > 1
    own = heads // 2
    steps = 8
    features = out_weight.shape[1] // n_head
    parts = pltpu.VMEM((n_head, tokens, features), BF16)
    state = pltpu.VMEM((own, DK, DV + DK), F32)
    return pl.pallas_call(
        functools.partial(finish_kernel, bits, n_head, steps),
        out_shape=jax.ShapeDtypeStruct((tokens, features), BF16),
        in_specs=[vmem, vmem, vmem, hbm, vmem, hbm],
        out_specs=vmem,
        scratch_shapes=[
            pltpu.VMEM((heads, DK, DV), BF16),
            pltpu.VMEM((tokens, heads * DV), BF16),
            state,
            state,
            state,
            pltpu.VMEM((bits, own, DK, DV + DK), BF16),
            pltpu.VMEM((bits, own, DK, DV + DK), BF16),
            pltpu.VMEM((own, DK, DV), BF16),
            pltpu.VMEM((own, DK, DV), BF16),
            pltpu.VMEM((own, DK, DV), BF16),
            parts,
            parts,
            parts,
            pltpu.SemaphoreType.DMA((bits + 1, own)),
            pltpu.SemaphoreType.DMA((bits + 1, own)),
            pltpu.SemaphoreType.DMA((n_head, steps)),
            pltpu.SemaphoreType.DMA((n_head, steps)),
            pltpu.SemaphoreType.DMA((n_head, steps)),
            pltpu.VMEM(gate_input.shape, BF16),
            pltpu.VMEM(out_weight.shape, BF16),
            pltpu.SemaphoreType.DMA((2,)),
        ],
        compiler_params=pltpu.CompilerParams(
            vmem_limit_bytes=48 * 2**20, collective_id=0, has_side_effects=True
        ),
        name="finish",
    )(out, qeff, trans, gate_input, norm_gain.reshape(1, DV), out_weight)


def solution(mesh):
    return jax.shard_map(
        body,
        mesh=mesh,
        in_specs=(
            P("ctx", "head"), P("ctx", "head"), P("ctx", "head"),
            P(None, "head"), P(None, "head"), P(None, "head"),
            P("head", "ctx"), P("head", "ctx"), P("ctx", "head"),
            P(), P("head", None),
        ),
        out_specs=P("ctx", "head"),
        check_vma=False,
    )
```

```python
import functools

import jax
import jax.numpy as jnp
from jax import lax
from jax.experimental import pallas as pl
from jax.experimental.pallas import tpu as pltpu
from jax.sharding import PartitionSpec as P

DK = 128
DV = 128
CONV = 4
BLOCK = 64
CHUNK = 2 * BLOCK
RIM = 16
F32 = jnp.float32
BF16 = jnp.bfloat16


def mm(a, b):
    return jnp.dot(a.astype(BF16), b.astype(BF16), preferred_element_type=F32)


def mm_nt(a, b):
    return lax.dot_general(
        a.astype(BF16), b.astype(BF16), (((1,), (1,)), ((), ())), preferred_element_type=F32
    )


def silu(x):
    return x / (1.0 + jnp.exp(-x))


def iota(shape, dim):
    return lax.broadcasted_iota(jnp.int32, shape, dim)


def conv_part(tail, rows, taps):
    whole = jnp.concatenate([tail, rows], 0)
    first = 8 - (CONV - 1)
    total = taps[0:1] * whole[first : first + CHUNK]
    for j in range(1, CONV):
        total = total + taps[j : j + 1] * whole[first + j : first + j + CHUNK]
    return silu(total)


def unit(x, scale):
    return x * (lax.rsqrt(jnp.sum(x * x, -1, keepdims=True) + 1e-06) * scale)


def local_kernel(
    q_ref, k_ref, v_ref, rim_ref, cq_ref, ck_ref, cv_ref, dec_ref, beta_ref,
    out_ref, qeff_ref, trans_ref,
    tail_ref, bd_ref, st_ref,
):
    tokens = q_ref.shape[0]
    key_heads = q_ref.shape[1] // DK
    heads = v_ref.shape[1] // DV
    ratio = heads // key_heads
    width = ratio * CHUNK
    qc, kc = q_ref.shape[1], k_ref.shape[1]

    tail_ref[...] = rim_ref[...].astype(F32)[RIM - 8 :]
    bd_ref[...] = (
        iota((width, width), 0) // BLOCK == iota((width, width), 1) // BLOCK
    ).astype(F32).astype(BF16)
    for h in range(heads):
        st_ref[h] = jnp.concatenate(
            [jnp.zeros((DK, DV), F32), (iota((DK, DK), 0) == iota((DK, DK), 1)).astype(F32)], 1
        )

    def diag(value):
        return jnp.concatenate([value] * (width // BLOCK), 0) * bd_ref[...]

    def step(c, unused):
        at = pl.ds(pl.multiple_of(c * CHUNK, CHUNK), CHUNK)
        row = iota((BLOCK, width), 0)
        lane = iota((BLOCK, width), 1)
        col = lane % BLOCK
        half = iota((BLOCK, CHUNK), 1) < BLOCK
        row1, col1 = iota((BLOCK, CHUNK), 0), iota((BLOCK, CHUNK), 1) % BLOCK
        eye = (row == col).astype(F32)

        dec = dec_ref[:, at]
        beta = beta_ref[:, at]
        tri = (
            (iota((CHUNK, CHUNK), 0) <= iota((CHUNK, CHUNK), 1))
            & (iota((CHUNK, CHUNK), 0) // BLOCK == iota((CHUNK, CHUNK), 1) // BLOCK)
        ).astype(F32)
        cum = jnp.dot(dec, tri, precision=lax.Precision.HIGHEST, preferred_element_type=F32)
        last = jnp.where(
            iota((heads, CHUNK), 1) < BLOCK, cum[:, BLOCK - 1 : BLOCK], cum[:, CHUNK - 1 : CHUNK]
        )
        grow = jnp.exp(cum)
        rows = jnp.concatenate(
            [cum, beta, beta * grow, grow, jnp.exp(last - cum)], 0
        )
        cols = jnp.transpose(
            jnp.concatenate([rows, jnp.zeros((CHUNK - rows.shape[0], CHUNK), F32)], 0)
        )

        def column(kind, h):
            return cols[:, kind * heads + h : kind * heads + h + 1]

        def compact(x):
            return jnp.where(half, x[:BLOCK], x[BLOCK:])

        def conv(ref, taps_ref, offset, part):
            s = pl.ds(part * DK, DK)
            t = pl.ds(offset + part * DK, DK)
            new = ref[at, s].astype(F32)
            result = conv_part(tail_ref[:, t], new, taps_ref[:, s].astype(F32))
            tail_ref[:, t] = new[CHUNK - 8 :]
            return result

        queries, keys, lowers, scores, values = [], [], [], [], []
        for kh in range(key_heads):
            q = unit(conv(q_ref, cq_ref, 0, kh), DK ** (-0.5))
            k = unit(conv(k_ref, ck_ref, qc, kh), 1.0)
            kk = compact(mm_nt(k, k))
            qk = compact(mm_nt(q, k))
            low = []
            for g in range(ratio):
                h = kh * ratio + g
                values.append(conv(v_ref, cv_ref, qc + kc, h))
                cc = compact(jnp.broadcast_to(column(0, h), (CHUNK, CHUNK)))
                bc = compact(jnp.broadcast_to(column(1, h), (CHUNK, CHUNK)))
                spread = jnp.exp(jnp.where(row1 >= col1, cc - cum[h : h + 1], 0.0))
                low.append(jnp.where(row1 > col1, bc * kk * spread, 0.0))
                scores.append(jnp.where(row1 >= col1, qk * spread, 0.0).astype(BF16))
            lowers.append(jnp.concatenate(low, 1))
            queries.append(q)
            keys.append(k)

        inverse = [eye - jnp.where(row // 2 == col // 2, low, 0.0) for low in lowers]
        size = 2
        while size < BLOCK:
            off = (row // (2 * size) == col // (2 * size)) & (row // size > col // size)
            left = [
                mm(x, diag(jnp.where(off, low, 0.0).astype(BF16)))
                for x, low in zip(inverse, lowers)
            ]
            inverse = [x - mm(p, diag(x.astype(BF16))) for x, p in zip(inverse, left)]
            size *= 2

        mixes = []
        for kh in range(key_heads):
            rhs = []
            for g in range(ratio):
                h = kh * ratio + g
                rhs.append(
                    jnp.concatenate([column(2, h) * keys[kh], column(1, h) * values[h]], 1)
                )
            mixes.append(mm(diag(inverse[kh].astype(BF16)), jnp.concatenate(rhs, 0)))

        firsts, seconds = [], []
        for h in range(heads):
            kh, g = h // ratio, h % ratio
            firsts.append((column(3, h) * queries[kh]).astype(BF16))
            turned = jnp.transpose(column(4, h) * keys[kh]).astype(BF16)
            seconds.append(jnp.concatenate([scores[h], turned], 0))

        for s in range(CHUNK // BLOCK):
            one = []
            for h in range(heads):
                kh, g = h // ratio, h % ratio
                mix = mixes[kh][g * CHUNK + s * BLOCK : g * CHUNK + (s + 1) * BLOCK]
                lhs = jnp.concatenate(
                    [mix[:, :DK].astype(BF16), firsts[h][s * BLOCK : (s + 1) * BLOCK]], 0
                )
                one.append((mm(lhs, st_ref[h]), mix[:, DK:]))
            for h in range(heads):
                r1, u = one[h]
                fresh = jnp.concatenate([u - r1[:BLOCK, :DV], -r1[:BLOCK, DV:]], 1).astype(BF16)
                zero = jnp.zeros_like(fresh)
                r2 = mm(seconds[h], jnp.concatenate([fresh, zero] if s == 0 else [zero, fresh], 0))
                result = r1[BLOCK:] + r2[:BLOCK]
                where = pl.ds(pl.multiple_of(c * CHUNK + s * BLOCK, BLOCK), BLOCK)
                out_ref[where, h * DV : (h + 1) * DV] = result[:, :DV]
                qeff_ref[where, h * DK : (h + 1) * DK] = result[:, DV:].astype(BF16)
                decay = jnp.exp(cum[h : h + 1, (s + 1) * BLOCK - 1 : (s + 1) * BLOCK])
                st_ref[h] = decay * st_ref[h] + r2[BLOCK:]
        return unused

    lax.fori_loop(0, tokens // CHUNK, step, 0)
    trans_ref[...] = st_ref[...].astype(BF16)


def local_entry(
    q_ref, k_ref, v_ref, dec_ref, beta_ref, rim_ref, taps_ref,
    out_ref, qeff_ref, trans_ref,
    tail_ref, bd_ref, st_ref, q_in, k_in, v_in, dec_in, beta_in, sem,
):
    pairs = ((q_ref, q_in), (k_ref, k_in), (v_ref, v_in), (dec_ref, dec_in), (beta_ref, beta_in))
    copies = [pltpu.make_async_copy(a, b, sem.at[i]) for i, (a, b) in enumerate(pairs)]
    for copy in copies:
        copy.start()
    for copy in copies:
        copy.wait()
    qc, kc = q_ref.shape[1], k_ref.shape[1]
    local_kernel(
        q_in, k_in, v_in, rim_ref,
        taps_ref.at[:, :qc], taps_ref.at[:, qc : qc + kc], taps_ref.at[:, qc + kc :],
        dec_in, beta_in, out_ref, qeff_ref, trans_ref, tail_ref, bd_ref, st_ref,
    )


def compose(later, earlier):
    moved = mm(later[:, DV:], earlier)
    return jnp.concatenate([moved[:, :DV] + later[:, :DV], moved[:, DV:]], 1)


def finish_kernel(
    bits, n_head, steps,
    out_ref, qeff_ref, trans_ref, gate_hbm, gain_ref, weight_hbm, mixed_ref,
    start_ref, hid_ref, total_ref, prefix_ref, low_ref, give_ref, got_ref, give_b_ref, got_b_ref,
    give_s_ref, part_ref, up_ref, down_ref,
    state_send, state_recv, part_send, up_recv, down_recv,
    gate_ref, weight_ref, in_sem,
):
    heads = trans_ref.shape[0]
    own = heads // 2
    tokens = out_ref.shape[0]
    rows = tokens // steps
    group = 4
    width = mixed_ref.shape[1]
    me, z = lax.axis_index("ctx"), lax.axis_index("head")
    core = me % 2
    first, other = core * own, (1 - core) * own

    def bit(b):
        return (me // 2**b) % 2

    def partner(b):
        return {"ctx": me + (1 - 2 * bit(b)) * 2**b}

    gate_copy = pltpu.make_async_copy(gate_hbm, gate_ref, in_sem.at[0])
    weight_copy = pltpu.make_async_copy(weight_hbm, weight_ref, in_sem.at[1])
    gate_copy.start()
    weight_copy.start()
    barrier = pltpu.get_barrier_semaphore()
    for b in range(bits):
        pl.semaphore_signal(
            barrier, inc=1, device_id=partner(b), device_id_type=pl.DeviceIdType.MESH
        )

    @pl.when(z > 0)
    def _():
        pl.semaphore_signal(
            barrier, inc=1, device_id={"head": z - 1}, device_id_type=pl.DeviceIdType.MESH
        )

    @pl.when(z < n_head - 1)
    def _():
        pl.semaphore_signal(
            barrier, inc=1, device_id={"head": z + 1}, device_id_type=pl.DeviceIdType.MESH
        )

    inner = (z > 0) & (z < n_head - 1)

    @pl.when(inner)
    def _():
        pl.semaphore_wait(barrier, bits + 2)

    @pl.when(jnp.logical_not(inner))
    def _():
        pl.semaphore_wait(barrier, bits + 1)

    def state_copy(b, i):
        if b == 0:
            src, dst = trans_ref.at[other + i], got_ref.at[0, i]
        elif b == bits:
            src, dst = give_s_ref.at[i], start_ref.at[first + i]
        elif b == bits - 1:
            src, dst = give_b_ref.at[i], got_b_ref.at[i]
        else:
            src, dst = give_ref.at[b, i], got_ref.at[b, i]
        return pltpu.make_async_remote_copy(
            src_ref=src, dst_ref=dst, send_sem=state_send.at[b, i], recv_sem=state_recv.at[b, i],
            device_id=partner(0 if b == bits else b), device_id_type=pl.DeviceIdType.MESH,
        )

    for i in range(own):
        state_copy(0, i).start()
    fresh = jnp.concatenate(
        [jnp.zeros((DK, DV), F32), (iota((DK, DK), 0) == iota((DK, DK), 1)).astype(F32)], 1
    )
    for i in range(own):
        state_copy(0, i).wait_recv()
        mine = trans_ref[first + i].astype(F32)
        got = got_ref[0, i].astype(F32)
        low = jnp.where(core == 0, mine, got)
        total = compose(jnp.where(core == 0, got, mine), low)
        low_ref[i] = low
        total_ref[i] = total
        prefix_ref[i] = fresh
        if bits - 1 == 1:
            give_b_ref[i] = total[:, :DV].astype(BF16)
        else:
            give_ref[1, i] = total.astype(BF16)
        state_copy(1, i).start()
    for b in range(1, bits - 1):
        for i in range(own):
            state_copy(b, i).wait_recv()
            got = got_ref[b, i].astype(F32)
            total = total_ref[i]

            @pl.when(bit(b) == 1)
            def _():
                prefix_ref[i] = compose(prefix_ref[i], got)

            total = compose(
                jnp.where(bit(b) == 1, total, got), jnp.where(bit(b) == 1, got, total)
            )
            total_ref[i] = total
            if b + 1 == bits - 1:
                give_b_ref[i] = total[:, :DV].astype(BF16)
            else:
                give_ref[b + 1, i] = total.astype(BF16)
            state_copy(b + 1, i).start()
    for i in range(own):
        state_copy(bits - 1, i).wait_recv()
        prefix = prefix_ref[i]
        moved = mm(prefix[:, DV:], got_b_ref[i]) + prefix[:, :DV]
        chip = jnp.where(bit(bits - 1) == 1, moved, prefix[:, :DV])
        low = low_ref[i]
        later = mm(low[:, DV:], chip) + low[:, :DV]
        start_ref[first + i] = jnp.where(core == 0, chip, later).astype(BF16)
        give_s_ref[i] = jnp.where(core == 0, later, chip).astype(BF16)
        state_copy(bits, i).start()
    for i in range(own):
        pltpu.make_async_remote_copy(
            src_ref=give_s_ref.at[i], dst_ref=start_ref.at[other + i],
            send_sem=state_send.at[bits, i], recv_sem=state_recv.at[bits, i],
            device_id=partner(0), device_id_type=pl.DeviceIdType.MESH,
        ).wait_recv()

    def piece(c):
        return pl.ds(pl.multiple_of(c * rows, rows), rows)

    def part_copy(up, d, c):
        at = piece(c)
        return pltpu.make_async_remote_copy(
            src_ref=part_ref.at[d, at], dst_ref=(up_ref if up else down_ref).at[d, at],
            send_sem=part_send.at[d, c], recv_sem=(up_recv if up else down_recv).at[d, c],
            device_id={"head": z + 1 if up else z - 1}, device_id_type=pl.DeviceIdType.MESH,
        )

    gain = gain_ref[...]
    gate_copy.wait()
    weight_copy.wait()
    for t in range(steps // group):
        at = slice(t * group * rows, (t + 1) * group * rows)
        for h in range(heads):
            cs = slice(h * DV, (h + 1) * DV)
            o = out_ref[at, cs] + mm(qeff_ref[at, cs], start_ref[h])
            n = o * lax.rsqrt(jnp.mean(o * o, -1, keepdims=True) + 1e-06)
            hid_ref[at, cs] = (n * gain * silu(gate_ref[at, cs].astype(F32))).astype(BF16)
        hidden = hid_ref[at, :]
        for d in range(n_head):
            part_ref[d, at, :] = mm(hidden, weight_ref[:, d * width : (d + 1) * width]).astype(BF16)

        def feed(up, targets):
            for c in range(t * group, (t + 1) * group):
                for d in targets:
                    if c > 0:
                        part_copy(up, d, c - 1).wait_send()
                    part_copy(up, d, c).start()

        @pl.when(z == 0)
        def _():
            feed(True, range(n_head - 1, 0, -1))

        @pl.when(z == n_head - 1)
        def _():
            feed(False, range(n_head - 1))

    def pass_on(up, d, c):
        inside = (z > 0) & (z < d) if up else (z < n_head - 1) & (z > d)

        @pl.when(inside)
        def _():
            part_copy(up, d, c).wait_recv()
            landed = (up_ref if up else down_ref)[d, piece(c), :].astype(F32)
            part_ref[d, piece(c), :] = (part_ref[d, piece(c), :].astype(F32) + landed).astype(BF16)
            part_copy(up, d, c).start()

    def ups(c):
        for d in range(n_head - 1, 0, -1):
            pass_on(True, d, c)

    def downs(c):
        for d in range(n_head - 1):
            pass_on(False, d, c)

    @pl.when(z < n_head // 2)
    def _():
        def lap(c, unused):
            ups(c)
            downs(c)
            return unused

        lax.fori_loop(0, steps, lap, 0)

    @pl.when(z >= n_head // 2)
    def _():
        def lap(c, unused):
            downs(c)
            ups(c)
            return unused

        lax.fori_loop(0, steps, lap, 0)

    def close(c, unused):
        for d in range(n_head):

            @pl.when(z == d)
            def _():
                total = part_ref[d, piece(c), :].astype(F32)
                if d > 0:
                    part_copy(True, d, c).wait_recv()
                    total = total + up_ref[d, piece(c), :].astype(F32)
                if d < n_head - 1:
                    part_copy(False, d, c).wait_recv()
                    total = total + down_ref[d, piece(c), :].astype(F32)
                mixed_ref[piece(c), :] = total.astype(BF16)

        return unused

    lax.fori_loop(0, steps, close, 0)

    for b in range(bits + 1):
        for i in range(own):
            state_copy(b, i).wait_send()
    for c in range(steps):
        for d in range(n_head):
            unsent = z != d
            if c < steps - 1:
                unsent = unsent & (z > 0) & (z < n_head - 1)

            @pl.when(unsent)
            def _():
                part_copy(True, d, c).wait_send()


def body(
    query_raw, key_raw, value_raw, conv_query, conv_key, conv_value,
    decay_log, write_beta, gate_input, norm_gain, out_weight,
):
    tokens = query_raw.shape[0]
    heads = value_raw.shape[1] // DV
    ratio = value_raw.shape[1] // key_raw.shape[1]
    channels = query_raw.shape[1] + key_raw.shape[1] + value_raw.shape[1]
    n_ctx, n_head = lax.axis_size("ctx"), lax.axis_size("head")
    rim = lax.ppermute(
        jnp.concatenate([x[tokens - RIM :] for x in (query_raw, key_raw, value_raw)], 1),
        "ctx",
        [(i, i + 1) for i in range(n_ctx - 1)],
    )
    vmem = pl.BlockSpec(memory_space=pltpu.VMEM)
    hbm = pl.BlockSpec(memory_space=pltpu.HBM)
    out, qeff, trans = pl.pallas_call(
        local_entry,
        out_shape=(
            jax.ShapeDtypeStruct((tokens, heads * DV), F32),
            jax.ShapeDtypeStruct((tokens, heads * DK), BF16),
            jax.ShapeDtypeStruct((heads, DK, DV + DK), BF16),
        ),
        in_specs=[hbm] * 5 + [vmem] * 2,
        out_specs=[vmem] * 3,
        scratch_shapes=[
            pltpu.VMEM((8, channels), F32),
            pltpu.VMEM((ratio * CHUNK, ratio * CHUNK), BF16),
            pltpu.VMEM((heads, DK, DV + DK), F32),
            *(
                pltpu.VMEM(x.shape, x.dtype)
                for x in (query_raw, key_raw, value_raw, decay_log, write_beta)
            ),
            pltpu.SemaphoreType.DMA((5,)),
        ],
        compiler_params=pltpu.CompilerParams(vmem_limit_bytes=48 * 2**20),
        name="local",
    )(
        query_raw, key_raw, value_raw, decay_log, write_beta, rim,
        jnp.concatenate([conv_query, conv_key, conv_value], 1).astype(F32),
    )
    bits = n_ctx.bit_length() - 1
    assert n_ctx == 2**bits and bits > 1
    own = heads // 2
    steps = 16
    features = out_weight.shape[1] // n_head
    parts = pltpu.VMEM((n_head, tokens, features), BF16)
    state = pltpu.VMEM((own, DK, DV + DK), F32)
    return pl.pallas_call(
        functools.partial(finish_kernel, bits, n_head, steps),
        out_shape=jax.ShapeDtypeStruct((tokens, features), BF16),
        in_specs=[vmem, vmem, vmem, hbm, vmem, hbm],
        out_specs=vmem,
        scratch_shapes=[
            pltpu.VMEM((heads, DK, DV), BF16),
            pltpu.VMEM((tokens, heads * DV), BF16),
            state,
            state,
            state,
            pltpu.VMEM((bits, own, DK, DV + DK), BF16),
            pltpu.VMEM((bits, own, DK, DV + DK), BF16),
            pltpu.VMEM((own, DK, DV), BF16),
            pltpu.VMEM((own, DK, DV), BF16),
            pltpu.VMEM((own, DK, DV), BF16),
            parts,
            parts,
            parts,
            pltpu.SemaphoreType.DMA((bits + 1, own)),
            pltpu.SemaphoreType.DMA((bits + 1, own)),
            pltpu.SemaphoreType.DMA((n_head, steps)),
            pltpu.SemaphoreType.DMA((n_head, steps)),
            pltpu.SemaphoreType.DMA((n_head, steps)),
            pltpu.VMEM(gate_input.shape, BF16),
            pltpu.VMEM(out_weight.shape, BF16),
            pltpu.SemaphoreType.DMA((2,)),
        ],
        compiler_params=pltpu.CompilerParams(
            vmem_limit_bytes=48 * 2**20, collective_id=0, has_side_effects=True
        ),
        name="finish",
    )(out, qeff, trans, gate_input, norm_gain.reshape(1, DV), out_weight)


def solution(mesh):
    return jax.shard_map(
        body,
        mesh=mesh,
        in_specs=(
            P("ctx", "head"), P("ctx", "head"), P("ctx", "head"),
            P(None, "head"), P(None, "head"), P(None, "head"),
            P("head", "ctx"), P("head", "ctx"), P("ctx", "head"),
            P(), P("head", None),
        ),
        out_specs=P("ctx", "head"),
        check_vma=False,
    )
```
